512 devices in a mesh: row: 64 (over y, x, core), col: 8 (over z).
Axes of the slice: x: 4, y: 8, z: 8, core: 2. Of those that a mesh axis runs over, the one named last changes fastest.
Arguments:
- samples: float32 [49152, 8192], P('row', 'col'), may hold values from -6 to 6
- start_basis: float32 [8192, 128], P('col'), may hold values from -6 to 6
Outputs:
- basis: float32 [49152, 128], P('row')
- upper: float32 [128, 128], replicated
- projected: float32 [8, 1024, 128], P('col', 'row')
The draws below stay inside these ranges and needn't reach their ends.
All inputs are finite; a program needn't handle non-finite values.
Results may differ from the reference program's by a relative error of at most 0.000075.
Values sent between devices are 32-bit elements; how exact they have to be, the bound alone decides.
No kernel may reach another device: no remote copies, remote signals or barrier semaphores. Data moves between devices by JAX's collectives and lax.ppermute only.
A program may use at most 64 MiB of HBM per device.

```python
import jax
import jax.numpy as jnp
from jax import lax

N = 8192
K = 128
TOTAL_ROWS = 49152
N_COL = 8


def shard_levels(own_key, extent, pieces, smallest, top_value):
    gain, own = 1.0, jax.random.fold_in(own_key, 6)
    for axis_at, parts in pieces:
        heights = jnp.exp(jax.random.uniform(jax.random.fold_in(own, axis_at), (parts,), jnp.float32, smallest / len(pieces), top_value / len(pieces)))
        gain = gain * jnp.repeat(heights, extent[axis_at] // parts).reshape([-1 if axis == axis_at else 1 for axis in range(len(extent))])
    return gain


def centred(own_key, extent, scale, most, shards=(), dtype=jnp.bfloat16):
    values = jax.random.normal(own_key, extent, jnp.float32) * scale
    if len(shards) > 0:
        values = shard_levels(own_key, extent, shards, -0.22, 0.18) * values
    return jnp.clip(values, min=-most, max=most).astype(dtype)


def setup_inputs(seed: int = 0) -> dict:
    keys = jax.random.split(jax.random.key(seed), 3)
    return {
        "samples": centred(keys[0], (TOTAL_ROWS, N), 1.0, 6.0, ((0, 64), (1, 8)), jnp.float32),
        "start_basis": centred(keys[1], (N, K), 1.0, 6.0, ((0, 8),), jnp.float32),
    }


def reference(samples, start_basis):
    high = lax.Precision.HIGHEST
    sketch = jnp.dot(samples.astype(jnp.float32), start_basis.astype(jnp.float32), precision=high, preferred_element_type=jnp.float32)
    gram = jnp.dot(sketch.T.astype(jnp.float32), sketch.astype(jnp.float32), precision=high, preferred_element_type=jnp.float32) / TOTAL_ROWS
    lower = jnp.linalg.cholesky(gram)
    basis = lax.linalg.triangular_solve(lower, sketch, left_side=False, lower=True, transpose_a=True)
    flat = jnp.dot(samples.T.astype(jnp.float32), basis.astype(jnp.float32), precision=high, preferred_element_type=jnp.float32) / jnp.sqrt(jnp.float32(TOTAL_ROWS))
    projected = flat.reshape(N_COL, N // N_COL, K)
    return (basis, lower.T, projected)
```

```python
import jax
import jax.numpy as jnp
from jax import lax
from jax.sharding import PartitionSpec as P

HIGH = lax.Precision.HIGH
HIGHEST = lax.Precision.HIGHEST


def times(left, right, precision):
    return jnp.dot(left, right, precision=precision, preferred_element_type=jnp.float32)


def exchange(parts, axis):
    return lax.all_to_all(parts, axis, 0, 0)


def body(samples, start_basis):
    rows, columns = samples.shape
    rank = start_basis.shape[1]
    n_row, n_col = lax.axis_size("row"), lax.axis_size("col")
    total = rows * n_row
    share, gram_share = columns // n_row, rank // n_row

    local = times(samples, start_basis, HIGH)
    chunk = exchange(local.reshape(n_col, rows // n_col, rank), "col").sum(0)
    sketch = exchange(jnp.broadcast_to(chunk, (n_col,) + chunk.shape), "col").reshape(rows, rank)

    gram = times(sketch.T, sketch, HIGHEST).reshape(n_row, 1, gram_share, rank)
    wide = times(samples.T, sketch, HIGH).reshape(n_row, share // gram_share, gram_share, rank)
    summed = exchange(jnp.concatenate([wide, gram], axis=1), "row").sum(0)
    mine = summed[:-1].reshape(share, rank)
    gram = exchange(jnp.broadcast_to(summed[-1], (n_row, gram_share, rank)), "row").reshape(rank, rank) / total

    lower = jnp.linalg.cholesky(gram)
    solve = lambda values: lax.linalg.triangular_solve(lower, values, left_side=False, lower=True, transpose_a=True)
    inverse = solve(jnp.eye(rank, dtype=jnp.float32))
    basis = times(sketch, inverse, HIGHEST)
    projected = times(mine, inverse, HIGHEST) * (1.0 / jnp.sqrt(jnp.float32(total)))
    return basis, lower.T, projected.reshape(1, share, rank)


def solution(mesh):
    in_specs = (P("row", "col"), P("col", None))
    out_specs = (P("row", None), P(), P("col", "row", None))
    return jax.shard_map(body, mesh=mesh, in_specs=in_specs, out_specs=out_specs, check_vma=False)
```

```python
import functools

import jax
import jax.numpy as jnp
from jax import lax
from jax.experimental import pallas as pl
from jax.experimental.pallas import tpu as pltpu
from jax.sharding import PartitionSpec as P

F32, BF16 = jnp.float32, jnp.bfloat16
HIGHEST = lax.Precision.HIGHEST
WHOLE = pl.BlockSpec(memory_space=pltpu.VMEM)
SUBLANES = 8


def halves(values):
    high = values.astype(BF16)
    return high, (values - high.astype(F32)).astype(BF16)


def dot(left, right, axes, precision=None):
    return lax.dot_general(
        left, right, (axes, ((), ())), precision=precision, preferred_element_type=F32
    )


def cost(flops, read, written):
    return pl.CostEstimate(flops=flops, bytes_accessed=4 * (read + written), transcendentals=0)


def split_dot(left, right_halves, axes):
    high, low = halves(left)
    both = dot(high, right_halves, axes) + dot(low, right_halves, axes)
    rank = right_halves.shape[1] // 2
    return both[:, :rank] + both[:, rank:]


def sketch_kernel(samples_ref, start_ref, local_ref, start_halves):
    @pl.when(pl.program_id(0) == 0)
    def _():
        high, low = halves(start_ref[...])
        rank = high.shape[1]
        start_halves[:, :rank] = high
        start_halves[:, rank:] = low

    local_ref[...] = split_dot(samples_ref[...], start_halves[...], ((1,), (0,)))


def sketch_product(samples, start_basis, step=128):
    rows, columns = samples.shape
    rank = start_basis.shape[1]
    return pl.pallas_call(
        sketch_kernel,
        grid=(rows // step,),
        in_specs=[
            pl.BlockSpec((step, columns), lambda i: (i, 0)),
            pl.BlockSpec((columns, rank), lambda i: (0, 0)),
        ],
        out_specs=pl.BlockSpec((step, rank), lambda i: (i, 0)),
        out_shape=jax.ShapeDtypeStruct((rows, rank), F32),
        scratch_shapes=[pltpu.VMEM((columns, 2 * rank), BF16)],
        cost_estimate=cost(8 * rows * columns * rank, rows * columns, rows * rank),
        name="sketch_product",
    )(samples, start_basis)


def sum_kernel(parts_ref, out_ref):
    total = parts_ref[0]
    for i in range(1, parts_ref.shape[0]):
        total = total + parts_ref[i]
    for i in range(out_ref.shape[0]):
        out_ref[i] = total


def sum_and_copy(parts):
    return pl.pallas_call(
        sum_kernel,
        in_specs=[WHOLE],
        out_specs=WHOLE,
        out_shape=jax.ShapeDtypeStruct(parts.shape, F32),
        cost_estimate=cost(parts.size, parts.size, parts.size),
        name="sum_and_copy",
    )(parts)


def gram_kernel(sketch_ref, gram_ref):
    sketch = sketch_ref[...]
    gram_ref[...] = dot(sketch, sketch, ((0,), (0,)), HIGHEST)


def gram_product(sketch):
    rows, rank = sketch.shape
    return pl.pallas_call(
        gram_kernel,
        in_specs=[WHOLE],
        out_specs=WHOLE,
        out_shape=jax.ShapeDtypeStruct((rank, rank), F32),
        cost_estimate=cost(2 * rows * rank * rank, rows * rank, rank * rank),
        name="gram_product",
    )(sketch)


def gram_sum_kernel(share, parts_ref, out_ref):
    rows = parts_ref.shape[0]
    total = parts_ref[:SUBLANES]
    for at in range(SUBLANES, rows, SUBLANES):
        total = total + parts_ref[at : at + SUBLANES]
    mine = total[:share]
    for at in range(share, SUBLANES, share):
        mine = mine + total[at : at + share]
    tile = jnp.concatenate([mine] * (SUBLANES // share), axis=0)
    for at in range(0, rows, SUBLANES):
        out_ref[at : at + SUBLANES] = tile


def gram_sum(parts, share):
    return pl.pallas_call(
        functools.partial(gram_sum_kernel, share),
        in_specs=[WHOLE],
        out_specs=WHOLE,
        out_shape=jax.ShapeDtypeStruct(parts.shape, F32),
        cost_estimate=cost(parts.size, parts.size, parts.size),
        name="gram_sum",
    )(parts)


def wide_kernel(samples_ref, sketch_ref, wide_ref, sketch_halves):
    @pl.when(pl.program_id(0) == 0)
    def _():
        high, low = halves(sketch_ref[...])
        rank = high.shape[1]
        sketch_halves[:, :rank] = high
        sketch_halves[:, rank:] = low

    wide_ref[...] = split_dot(samples_ref[...], sketch_halves[...], ((0,), (0,)))


def wide_product(samples, sketch, step=256):
    rows, columns = samples.shape
    rank = sketch.shape[1]
    return pl.pallas_call(
        wide_kernel,
        grid=(columns // step,),
        in_specs=[
            pl.BlockSpec((rows, step), lambda i: (0, i)),
            pl.BlockSpec((rows, rank), lambda i: (0, 0)),
        ],
        out_specs=pl.BlockSpec((step, rank), lambda i: (i, 0)),
        out_shape=jax.ShapeDtypeStruct((columns, rank), F32),
        scratch_shapes=[pltpu.VMEM((rows, 2 * rank), BF16)],
        cost_estimate=cost(8 * rows * columns * rank, rows * columns, columns * rank),
        name="wide_product",
    )(samples, sketch)


def factor_kernel(scale, gram_ref, sketch_ref, basis_ref, upper_ref, inverse_ref):
    size = gram_ref.shape[0]
    count = size // SUBLANES
    lane = lax.broadcasted_iota(jnp.int32, (SUBLANES, size), 1)
    sub = lax.broadcasted_iota(jnp.int32, (SUBLANES, size), 0)
    down = lambda values, row: jnp.broadcast_to(values[row : row + 1, :], values.shape)
    across = lambda values, column: jnp.broadcast_to(values[:, column : column + 1], values.shape)
    tiles = [gram_ref[SUBLANES * t : SUBLANES * (t + 1), :] * scale for t in range(count)]
    for j in range(count):
        base = SUBLANES * j
        inside = (lane >= base) & (lane < base + SUBLANES)
        rest = range(j + 1, count)
        own = [across(tiles[j], base + k) for k in range(SUBLANES)]
        below = {t: [across(tiles[t], base + k) for k in range(SUBLANES)] for t in rest}
        panel = jnp.where(inside, jnp.where(lane - base == sub, 1.0, 0.0), tiles[j])
        for t in rest:
            tiles[t] = jnp.where(inside, 0.0, tiles[t])
        diagonal = jnp.ones_like(panel)
        for k in range(SUBLANES):
            pivot = down(own[k], k)
            diagonal = jnp.where(sub == k, pivot, diagonal)
            reciprocal = 1.0 / pivot
            heads = {i: down(own[i], k) for i in range(k + 1, SUBLANES)}
            row = down(panel, k)
            factor = jnp.where(sub > k, own[k] * reciprocal, 0.0)
            for i in heads:
                own[i] = own[i] - factor * heads[i]
            panel = panel - factor * row
            for t in rest:
                factor = below[t][k] * reciprocal
                for i in heads:
                    below[t][i] = below[t][i] - factor * heads[i]
                tiles[t] = tiles[t] - factor * row
        root = lax.rsqrt(diagonal)
        done = panel * root
        block = jnp.zeros_like(panel)
        for k in range(SUBLANES):
            block = jnp.where(lane == base + k, own[k] * root, block)
        block = jnp.where(lane - base >= sub, block, 0.0)
        here = slice(base, base + SUBLANES)
        upper_ref[here, :] = jnp.where(lane >= base + SUBLANES, done, block)
        inverse_ref[here, :] = jnp.where(lane < base + SUBLANES, done, 0.0)
    basis_ref[...] = dot(sketch_ref[...], inverse_ref[...], ((1,), (1,)), HIGHEST)


def factor(gram, sketch, scale):
    rows, rank = sketch.shape
    square = jax.ShapeDtypeStruct(gram.shape, F32)
    return pl.pallas_call(
        functools.partial(factor_kernel, scale),
        in_specs=[WHOLE, WHOLE],
        out_specs=(WHOLE,) * 3,
        out_shape=(jax.ShapeDtypeStruct(sketch.shape, F32), square, square),
        cost_estimate=cost(50 * 2 * rows * rank * rank, rows * rank, rows * rank),
        name="factor",
    )(gram, sketch)


def project_kernel(scale, parts_ref, inverse_ref, out_ref):
    total = parts_ref[0]
    for i in range(1, parts_ref.shape[0]):
        total = total + parts_ref[i]
    out_ref[0] = dot(total, inverse_ref[...], ((1,), (1,)), HIGHEST) * scale


def project(parts, inverse, scale):
    return pl.pallas_call(
        functools.partial(project_kernel, scale),
        in_specs=[WHOLE, WHOLE],
        out_specs=WHOLE,
        out_shape=jax.ShapeDtypeStruct((1,) + parts.shape[1:], F32),
        cost_estimate=cost(parts.size, parts.size, inverse.size),
        name="project",
    )(parts, inverse)


def exchange(parts, axis):
    return lax.all_to_all(parts, axis, 0, 0)


def body(samples, start_basis):
    rows, columns = samples.shape
    rank = start_basis.shape[1]
    n_row, n_col = lax.axis_size("row"), lax.axis_size("col")
    total = rows * n_row
    share, gram_share = columns // n_row, rank // n_row

    local = sketch_product(samples, start_basis)
    chunks = sum_and_copy(exchange(local.reshape(n_col, rows // n_col, rank), "col"))
    sketch = exchange(chunks, "col").reshape(rows, rank)

    gram = exchange(gram_product(sketch).reshape(n_row, gram_share, rank), "row")
    wide = wide_product(samples, sketch).reshape(n_row, share, rank)
    gram = gram_sum(gram.reshape(rank, rank), gram_share)
    gram = exchange(gram.reshape(n_row, gram_share, rank), "row").reshape(rank, rank)
    wide = exchange(wide, "row")
    basis, upper, inverse = factor(gram, sketch, 1.0 / total)
    return basis, upper, project(wide, inverse, 1.0 / total**0.5)


def solution(mesh):
    in_specs = (P("row", "col"), P("col", None))
    out_specs = (P("row", None), P(), P("col", "row", None))
    return jax.shard_map(body, mesh=mesh, in_specs=in_specs, out_specs=out_specs, check_vma=False)
```

```python
import functools

import jax
import jax.numpy as jnp
from jax import lax
from jax.experimental import pallas as pl
from jax.experimental.pallas import tpu as pltpu
from jax.sharding import PartitionSpec as P

F32, BF16 = jnp.float32, jnp.bfloat16
HIGHEST = lax.Precision.HIGHEST
WHOLE = pl.BlockSpec(memory_space=pltpu.VMEM)
SUBLANES = 8
LIMIT = 12 * 2**20


def halves(values):
    high = values.astype(BF16)
    return high, (values - high.astype(F32)).astype(BF16)


def dot(left, right, axes, precision=None):
    return lax.dot_general(
        left, right, (axes, ((), ())), precision=precision, preferred_element_type=F32
    )


def cost(flops, read, written):
    return pl.CostEstimate(flops=flops, bytes_accessed=4 * (read + written), transcendentals=0)


def split_dot(left, right_halves, axes):
    high, low = halves(left)
    both = dot(high, right_halves, axes) + dot(low, right_halves, axes)
    rank = right_halves.shape[1] // 2
    return both[:, :rank] + both[:, rank:]


def sketch_kernel(step, samples_ref, start_ref, local_ref, held_ref, start, start_halves, sems, start_sem):
    rows = local_ref.shape[0]
    rank = local_ref.shape[1]
    first = pltpu.make_async_copy(start_ref, start, start_sem)
    first.start()
    copies = []
    for i in range(rows // step):
        at = pl.ds(i * step, step)
        copies.append(pltpu.make_async_copy(samples_ref.at[at], held_ref.at[at], sems.at[i]))
        copies[-1].start()
    first.wait()
    high, low = halves(start[...])
    start_halves[:, :rank] = high
    start_halves[:, rank:] = low
    for i, copy in enumerate(copies):
        copy.wait()
        at = pl.ds(i * step, step)
        local_ref[at] = split_dot(held_ref[at], start_halves[...], ((1,), (0,)))


def sketch_product(samples, start_basis, step=128):
    rows, columns = samples.shape
    rank = start_basis.shape[1]
    return pl.pallas_call(
        functools.partial(sketch_kernel, step),
        in_specs=[pl.BlockSpec(memory_space=pltpu.HBM)] * 2,
        out_specs=(WHOLE, WHOLE),
        out_shape=(
            jax.ShapeDtypeStruct((rows, rank), F32),
            jax.ShapeDtypeStruct((rows, columns), F32),
        ),
        scratch_shapes=[
            pltpu.VMEM((columns, rank), F32),
            pltpu.VMEM((columns, 2 * rank), BF16),
            pltpu.SemaphoreType.DMA((rows // step,)),
            pltpu.SemaphoreType.DMA,
        ],
        compiler_params=pltpu.CompilerParams(vmem_limit_bytes=LIMIT),
        cost_estimate=cost(8 * rows * columns * rank, rows * columns, rows * rank),
        name="sketch_product",
    )(samples, start_basis)


def sum_kernel(parts_ref, out_ref):
    total = parts_ref[0]
    for i in range(1, parts_ref.shape[0]):
        total = total + parts_ref[i]
    for i in range(out_ref.shape[0]):
        out_ref[i] = total


def sum_and_copy(parts):
    return pl.pallas_call(
        sum_kernel,
        in_specs=[WHOLE],
        out_specs=WHOLE,
        out_shape=jax.ShapeDtypeStruct(parts.shape, F32),
        compiler_params=pltpu.CompilerParams(vmem_limit_bytes=LIMIT),
        cost_estimate=cost(parts.size, parts.size, parts.size),
        name="sum_and_copy",
    )(parts)


def gram_kernel(share, sketch_ref, out_ref):
    sketch = sketch_ref[...]
    gram = dot(sketch, sketch, ((0,), (0,)), HIGHEST)
    for at in range(0, gram.shape[0], share):
        part = gram[at : at + share]
        out_ref[2 * at : 2 * at + 2 * share] = jnp.concatenate([part, part], axis=0)


def gram_product(sketch, share):
    rows, rank = sketch.shape
    return pl.pallas_call(
        functools.partial(gram_kernel, share),
        in_specs=[WHOLE],
        out_specs=WHOLE,
        out_shape=jax.ShapeDtypeStruct((2 * rank, rank), F32),
        compiler_params=pltpu.CompilerParams(vmem_limit_bytes=LIMIT),
        cost_estimate=cost(2 * rows * rank * rank, rows * rank, rank * rank),
        name="gram_product",
    )(sketch)


def wide_kernel(step, share, samples_ref, sketch_ref, own_ref, other_ref, sketch_halves):
    core = lax.axis_index("core")
    rank = sketch_ref.shape[1]
    high, low = halves(sketch_ref[...])
    sketch_halves[:, :rank] = high
    sketch_halves[:, rank:] = low
    for at in range(0, samples_ref.shape[1], step):
        wide = split_dot(samples_ref[:, at : at + step], sketch_halves[...], ((0,), (0,)))
        for chip in range(step // (2 * share)):
            pair = [wide[share * (2 * chip + i) : share * (2 * chip + i + 1)] for i in range(2)]
            here = slice(at // 2 + share * chip, at // 2 + share * (chip + 1))
            own_ref[here] = jnp.where(core == 0, pair[0], pair[1])
            other_ref[here] = jnp.where(core == 0, pair[1], pair[0])


def wide_product(samples, sketch, share, step=256):
    rows, columns = samples.shape
    rank = sketch.shape[1]
    half = jax.ShapeDtypeStruct((columns // 2, rank), F32)
    return pl.pallas_call(
        functools.partial(wide_kernel, step, share),
        in_specs=[WHOLE, WHOLE],
        out_specs=(WHOLE, WHOLE),
        out_shape=(half, half),
        scratch_shapes=[pltpu.VMEM((rows, 2 * rank), BF16)],
        compiler_params=pltpu.CompilerParams(vmem_limit_bytes=LIMIT),
        cost_estimate=cost(8 * rows * columns * rank, rows * columns, columns * rank),
        name="wide_product",
    )(samples, sketch)


def turned(values):
    return jnp.concatenate([values[4:], values[:4]], axis=0)


def pack_kernel(parts_ref, own_ref, received_ref, out_ref):
    tile = parts_ref[:SUBLANES]
    for at in range(SUBLANES, parts_ref.shape[0], SUBLANES):
        tile = tile + parts_ref[at : at + SUBLANES]
    gram = tile[:4] + tile[4:]
    gram = jnp.concatenate([gram, gram], axis=0)
    first = lax.broadcasted_iota(jnp.int32, gram.shape, 0) < 4
    for pair in range(out_ref.shape[0] // 40):
        rows = [slice(32 * pair + 8 * i, 32 * pair + 8 * i + 8) for i in range(4)]
        a, b, c, d = [own_ref[here] + received_ref[here] for here in rows]
        c, d = turned(c), turned(d)
        tiles = (a, b, jnp.where(first, gram, c), jnp.where(first, c, d), jnp.where(first, d, gram))
        for i, value in enumerate(tiles):
            out_ref[40 * pair + 8 * i : 40 * pair + 8 * i + 8] = value


def pack(parts, own, received):
    rows = own.shape[0] // 16 * 20
    return pl.pallas_call(
        pack_kernel,
        in_specs=[WHOLE] * 3,
        out_specs=WHOLE,
        out_shape=jax.ShapeDtypeStruct((rows, own.shape[1]), F32),
        compiler_params=pltpu.CompilerParams(vmem_limit_bytes=LIMIT),
        cost_estimate=cost(parts.size, parts.size, rows * 128),
        name="pack",
    )(parts, own, received)


def factor_kernel(total, parts_ref, sketch_ref, basis_ref, upper_ref, projected_ref, inverse_ref):
    size = upper_ref.shape[0]
    count = size // SUBLANES
    lane = lax.broadcasted_iota(jnp.int32, (SUBLANES, size), 1)
    sub = lax.broadcasted_iota(jnp.int32, (SUBLANES, size), 0)
    down = lambda values, row: jnp.broadcast_to(values[row : row + 1, :], values.shape)
    across = lambda values, column: jnp.broadcast_to(values[:, column : column + 1], values.shape)
    half = sub < 4
    piece = lambda at: parts_ref[at : at + SUBLANES]
    tiles = [jnp.where(half, piece(40 * t + 16), piece(40 * t + 32)) / total for t in range(count)]
    for j in range(count):
        base = SUBLANES * j
        inside = (lane >= base) & (lane < base + SUBLANES)
        rest = range(j + 1, count)
        own = [across(tiles[j], base + k) for k in range(SUBLANES)]
        below = {t: [across(tiles[t], base + k) for k in range(SUBLANES)] for t in rest}
        panel = jnp.where(inside, jnp.where(lane - base == sub, 1.0, 0.0), tiles[j])
        for t in rest:
            tiles[t] = jnp.where(inside, 0.0, tiles[t])
        diagonal = jnp.ones_like(panel)
        for k in range(SUBLANES):
            pivot = down(own[k], k)
            diagonal = jnp.where(sub == k, pivot, diagonal)
            reciprocal = 1.0 / pivot
            heads = {i: down(own[i], k) for i in range(k + 1, SUBLANES)}
            row = down(panel, k)
            factor = jnp.where(sub > k, own[k] * reciprocal, 0.0)
            for i in heads:
                own[i] = own[i] - factor * heads[i]
            panel = panel - factor * row
            for t in rest:
                factor = below[t][k] * reciprocal
                for i in heads:
                    below[t][i] = below[t][i] - factor * heads[i]
                tiles[t] = tiles[t] - factor * row
        root = lax.rsqrt(diagonal)
        done = panel * root
        block = jnp.zeros_like(panel)
        for k in range(SUBLANES):
            block = jnp.where(lane == base + k, own[k] * root, block)
        block = jnp.where(lane - base >= sub, block, 0.0)
        here = slice(base, base + SUBLANES)
        upper_ref[here, :] = jnp.where(lane >= base + SUBLANES, done, block)
        inverse_ref[here, :] = jnp.where(lane < base + SUBLANES, done, 0.0)
    basis_ref[...] = dot(sketch_ref[...], inverse_ref[...], ((1,), (1,)), HIGHEST)
    a, b, c, d, e = [sum(piece(40 * t + 8 * i) for t in range(1, count)) + piece(8 * i) for i in range(5)]
    odd = [turned(jnp.where(half, d, c)), turned(jnp.where(half, e, d))]
    mine = jnp.concatenate([a + odd[0], b + odd[1]], axis=0)
    projected_ref[0] = dot(mine, inverse_ref[...], ((1,), (1,)), HIGHEST) * (1.0 / total**0.5)


def factor(parts, sketch, total):
    rows, rank = sketch.shape
    return pl.pallas_call(
        functools.partial(factor_kernel, total),
        in_specs=[WHOLE, WHOLE],
        out_specs=(WHOLE,) * 3,
        out_shape=(
            jax.ShapeDtypeStruct(sketch.shape, F32),
            jax.ShapeDtypeStruct((rank, rank), F32),
            jax.ShapeDtypeStruct((1, 16, rank), F32),
        ),
        scratch_shapes=[pltpu.VMEM((rank, rank), F32)],
        compiler_params=pltpu.CompilerParams(vmem_limit_bytes=LIMIT),
        cost_estimate=cost(50 * 2 * rows * rank * rank, rows * rank, rows * rank),
        name="factor",
    )(parts, sketch)


def exchange(parts, axis):
    return lax.all_to_all(parts, axis, 0, 0)


def body(samples, start_basis):
    rows, columns = samples.shape
    rank = start_basis.shape[1]
    chips, cores, n_col = lax.axis_size("chip"), lax.axis_size("core"), lax.axis_size("col")
    total = rows * chips * cores
    share, gram_share = columns // (chips * cores), rank // chips

    local, samples = sketch_product(samples, start_basis)
    chunks = sum_and_copy(exchange(local.reshape(n_col, rows // n_col, rank), "col"))
    sketch = exchange(chunks, "col").reshape(rows, rank)

    gram, late = lax.optimization_barrier((gram_product(sketch, gram_share), sketch))
    gram = exchange(gram.reshape(chips * cores, gram_share, rank), ("chip", "core")).reshape(2 * rank, rank)
    own, other = wide_product(samples, late, share)
    received = lax.ppermute(other, "core", [(0, 1), (1, 0)])
    packed = pack(gram, own, received).reshape(chips, -1, gram_share, rank)
    parts = exchange(packed, "chip").reshape(-1, rank)
    return factor(parts, sketch, float(total))


def solution(mesh):
    devices = mesh.devices
    split = jax.sharding.Mesh(
        devices.reshape(devices.shape[0] // 2, 2, devices.shape[1]), ("chip", "core", "col")
    )
    row = ("chip", "core")
    in_specs = (P(row, "col"), P("col", None))
    out_specs = (P(row, None), P(), P("col", row, None))
    return jax.shard_map(body, mesh=split, in_specs=in_specs, out_specs=out_specs, check_vma=False)
```

```python
import functools

import jax
import jax.numpy as jnp
from jax import lax
from jax.experimental import pallas as pl
from jax.experimental.pallas import tpu as pltpu
from jax.sharding import PartitionSpec as P

F32, BF16 = jnp.float32, jnp.bfloat16
HIGHEST = lax.Precision.HIGHEST
WHOLE = pl.BlockSpec(memory_space=pltpu.VMEM)
SUBLANES = 8
LIMIT = 12 * 2**20


def halves(values):
    high = values.astype(BF16)
    return high, (values - high.astype(F32)).astype(BF16)


def dot(left, right, axes, precision=None):
    return lax.dot_general(
        left, right, (axes, ((), ())), precision=precision, preferred_element_type=F32
    )


def cost(flops, read, written):
    return pl.CostEstimate(flops=flops, bytes_accessed=4 * (read + written), transcendentals=0)


def split_dot(left, right_halves, axes):
    high, low = halves(left)
    both = dot(high, right_halves, axes) + dot(low, right_halves, axes)
    rank = right_halves.shape[1] // 2
    return both[:, :rank] + both[:, rank:]


def sketch_kernel(step, block, samples_ref, start_ref, local_ref, held_ref, start, sems):
    rows, columns = held_ref.shape
    rank = local_ref.shape[1]
    copies = []
    for i in range(columns // step):
        at = pl.ds(i * step, step)
        pair = (
            pltpu.make_async_copy(start_ref.at[at], start.at[at], sems.at[0, i]),
            pltpu.make_async_copy(samples_ref.at[:, at], held_ref.at[:, at], sems.at[1, i]),
        )
        for copy in pair:
            copy.start()
        copies.append(pair)
    for i, pair in enumerate(copies):
        for copy in pair:
            copy.wait()
        at = slice(i * step, (i + 1) * step)
        right = jnp.concatenate(halves(start[at]), axis=1)
        for first in range(0, rows, block):
            here = slice(first, first + block)
            left = jnp.concatenate(halves(held_ref[here, at]), axis=0)
            both = dot(left, right, ((1,), (0,)))
            both = both[:block] + both[block:]
            both = both[:, :rank] + both[:, rank:]
            local_ref[here] = both if i == 0 else local_ref[here] + both


def sketch_product(samples, start_basis, step=256, block=128):
    rows, columns = samples.shape
    rank = start_basis.shape[1]
    samples, start_basis = (
        pltpu.with_memory_space_constraint(values, pltpu.HBM) for values in (samples, start_basis)
    )
    return pl.pallas_call(
        functools.partial(sketch_kernel, step, block),
        in_specs=[pl.BlockSpec(memory_space=pltpu.HBM)] * 2,
        out_specs=(WHOLE, WHOLE),
        out_shape=(
            jax.ShapeDtypeStruct((rows, rank), F32),
            jax.ShapeDtypeStruct((rows, columns), F32),
        ),
        scratch_shapes=[
            pltpu.VMEM((columns, rank), F32),
            pltpu.SemaphoreType.DMA((2, columns // step)),
        ],
        compiler_params=pltpu.CompilerParams(vmem_limit_bytes=LIMIT),
        cost_estimate=cost(8 * rows * columns * rank, rows * columns, rows * rank),
        name="sketch_product",
    )(samples, start_basis)


def sum_kernel(parts_ref, out_ref):
    total = parts_ref[0]
    for i in range(1, parts_ref.shape[0]):
        total = total + parts_ref[i]
    for i in range(out_ref.shape[0]):
        out_ref[i] = total


def sum_and_copy(parts):
    return pl.pallas_call(
        sum_kernel,
        in_specs=[WHOLE],
        out_specs=WHOLE,
        out_shape=jax.ShapeDtypeStruct(parts.shape, F32),
        compiler_params=pltpu.CompilerParams(vmem_limit_bytes=LIMIT),
        cost_estimate=cost(parts.size, parts.size, parts.size),
        name="sum_and_copy",
    )(parts)


def products_kernel(step, share, samples_ref, sketch_ref, own_ref, other_ref, sketch_halves):
    core = lax.axis_index("core")
    rank = sketch_ref.shape[1]

    def give(at, for_first, for_second):
        here = slice(at, at + for_first.shape[0])
        own_ref[here] = jnp.where(core == 0, for_first, for_second)
        other_ref[here] = jnp.where(core == 0, for_second, for_first)

    sketch = sketch_ref[...]
    gram = dot(sketch, sketch, ((0,), (0,)), HIGHEST)
    tiles = [gram[at : at + SUBLANES] for at in range(0, rank, SUBLANES)]
    packed = packed_tiles(tiles)
    middle = len(packed) // 2 + 1
    first, second = packed[:middle], packed[middle:]
    second += [jnp.zeros_like(gram[:SUBLANES])] * (len(first) - len(second))
    for i, pair in enumerate(zip(first, second)):
        give(samples_ref.shape[1] // 2 + SUBLANES * i, *pair)

    high, low = halves(sketch)
    sketch_halves[:, :rank] = high
    sketch_halves[:, rank:] = low
    for at in range(0, samples_ref.shape[1], step):
        wide = split_dot(samples_ref[:, at : at + step], sketch_halves[...], ((0,), (0,)))
        for begin in range(0, step, 2 * share):
            pair = [wide[begin + share * i : begin + share * (i + 1)] for i in range(2)]
            give((at + begin) // 2, *pair)


def packed_tiles(tiles):
    count, size = len(tiles), tiles[0].shape[1]
    lane = lax.broadcasted_iota(jnp.int32, tiles[0].shape, 1)
    packed = [tiles[0]]
    for t in range(1, count // 2):
        start = SUBLANES * t
        packed.append(jnp.where(lane >= start, tiles[t], pltpu.roll(tiles[count - t], start, 1)))
    return packed + [tiles[count // 2]]


def unpacked_tiles(packed):
    count, size = 2 * (len(packed) - 1), packed[0].shape[1]
    tiles = list(packed) + [None] * (count - len(packed))
    for t in range(1, count // 2):
        tiles[count - t] = pltpu.roll(packed[t], size - SUBLANES * t, 1)
    upper = jnp.concatenate(tiles, axis=0)
    row = lax.broadcasted_iota(jnp.int32, upper.shape, 0)
    lane = lax.broadcasted_iota(jnp.int32, upper.shape, 1)
    whole = jnp.where(lane >= row // SUBLANES * SUBLANES, upper, upper.T)
    return [whole[at : at + SUBLANES] for at in range(0, size, SUBLANES)]


def gram_rows(rank):
    return SUBLANES * (rank // SUBLANES // 4 + 1)


def products(samples, sketch, share, step=256):
    rows, columns = samples.shape
    rank = sketch.shape[1]
    half = jax.ShapeDtypeStruct((columns // 2 + gram_rows(rank), rank), F32)
    return pl.pallas_call(
        functools.partial(products_kernel, step, share),
        in_specs=[WHOLE, WHOLE],
        out_specs=(WHOLE, WHOLE),
        out_shape=(half, half),
        scratch_shapes=[pltpu.VMEM((rows, 2 * rank), BF16)],
        compiler_params=pltpu.CompilerParams(vmem_limit_bytes=LIMIT),
        cost_estimate=cost(8 * rows * columns * rank, rows * columns, columns * rank),
        name="products",
    )(samples, sketch)


def added(refs, at, rows):
    total = refs[0][at : at + rows]
    for ref in refs[1:]:
        total = total + ref[at : at + rows]
    return total


def spread_kernel(share, inner, outer, gram, *refs):
    *parts, out_ref = refs
    last = added(parts, outer * inner * share, gram)
    size = outer * share + gram
    for i in range(inner):
        for o in range(outer):
            here = size * i + share * o
            out_ref[here : here + share] = added(parts, (o * inner + i) * share, share)
        out_ref[size * (i + 1) - gram : size * (i + 1)] = last


def spread(parts, share, inner, gram):
    rows, rank = parts[0].shape
    outer = (rows - gram) // share // inner
    size = outer * share + gram
    out = pl.pallas_call(
        functools.partial(spread_kernel, share, inner, outer, gram),
        in_specs=[WHOLE] * len(parts),
        out_specs=WHOLE,
        out_shape=jax.ShapeDtypeStruct((inner * size, rank), F32),
        compiler_params=pltpu.CompilerParams(vmem_limit_bytes=LIMIT),
        cost_estimate=cost(rows * rank, rows * rank, inner * size * rank),
        name="spread",
    )(*parts)
    return out.reshape(inner, size, rank)


def respread_kernel(share, count, gram, parts_ref, out_ref):
    parts = [parts_ref.at[i] for i in range(parts_ref.shape[0])]
    last = added(parts, count * share, gram)
    for i in range(count):
        out_ref[i, :share] = added(parts, i * share, share)
        out_ref[i, share:] = last


def respread(parts, share, gram):
    count = (parts.shape[1] - gram) // share
    rank = parts.shape[2]
    return pl.pallas_call(
        functools.partial(respread_kernel, share, count, gram),
        in_specs=[WHOLE],
        out_specs=WHOLE,
        out_shape=jax.ShapeDtypeStruct((count, share + gram, rank), F32),
        compiler_params=pltpu.CompilerParams(vmem_limit_bytes=LIMIT),
        cost_estimate=cost(parts.size, parts.size, parts.size),
        name="respread",
    )(parts)


def finish_kernel(parts_ref, mine_ref, gram_ref):
    parts = [parts_ref.at[i] for i in range(parts_ref.shape[0])]
    share, gram = mine_ref.shape[0], gram_ref.shape[0]
    mine_ref[...] = added(parts, 0, share)
    gram_ref[...] = added(parts, share, gram)


def finish(parts, share):
    rows, rank = parts.shape[1:]
    return pl.pallas_call(
        finish_kernel,
        in_specs=[WHOLE],
        out_specs=(WHOLE, WHOLE),
        out_shape=(
            jax.ShapeDtypeStruct((share, rank), F32),
            jax.ShapeDtypeStruct((rows - share, rank), F32),
        ),
        compiler_params=pltpu.CompilerParams(vmem_limit_bytes=LIMIT),
        cost_estimate=cost(parts.size, parts.size, rows * rank),
        name="finish",
    )(parts)


def factor_kernel(
    total, packed_ref, mine_ref, sketch_ref, basis_ref, upper_ref, projected_ref, inverse_ref
):
    size = upper_ref.shape[0]
    count = size // SUBLANES
    lane = lax.broadcasted_iota(jnp.int32, (SUBLANES, size), 1)
    sub = lax.broadcasted_iota(jnp.int32, (SUBLANES, size), 0)
    down = lambda values, row: jnp.broadcast_to(values[row : row + 1, :], values.shape)
    across = lambda values, column: jnp.broadcast_to(values[:, column : column + 1], values.shape)
    packed = [packed_ref[SUBLANES * i : SUBLANES * (i + 1)] for i in range(count // 2 + 1)]
    tiles = [tile / total for tile in unpacked_tiles(packed)]
    for j in range(count):
        base = SUBLANES * j
        inside = (lane >= base) & (lane < base + SUBLANES)
        rest = range(j + 1, count)
        own = [across(tiles[j], base + k) for k in range(SUBLANES)]
        below = {t: [across(tiles[t], base + k) for k in range(SUBLANES)] for t in rest}
        panel = jnp.where(inside, jnp.where(lane - base == sub, 1.0, 0.0), tiles[j])
        for t in rest:
            tiles[t] = jnp.where(inside, 0.0, tiles[t])
        diagonal = jnp.ones_like(panel)
        for k in range(SUBLANES):
            pivot = down(own[k], k)
            diagonal = jnp.where(sub == k, pivot, diagonal)
            reciprocal = 1.0 / pivot
            heads = {i: down(own[i], k) for i in range(k + 1, SUBLANES)}
            row = down(panel, k)
            factor = jnp.where(sub > k, own[k] * reciprocal, 0.0)
            for i in heads:
                own[i] = own[i] - factor * heads[i]
            panel = panel - factor * row
            for t in rest:
                factor = below[t][k] * reciprocal
                for i in heads:
                    below[t][i] = below[t][i] - factor * heads[i]
                tiles[t] = tiles[t] - factor * row
        root = lax.rsqrt(diagonal)
        done = panel * root
        block = jnp.zeros_like(panel)
        for k in range(SUBLANES):
            block = jnp.where(lane == base + k, own[k] * root, block)
        block = jnp.where(lane - base >= sub, block, 0.0)
        here = slice(base, base + SUBLANES)
        upper_ref[here, :] = jnp.where(lane >= base + SUBLANES, done, block)
        inverse_ref[here, :] = jnp.where(lane < base + SUBLANES, done, 0.0)
    basis_ref[...] = dot(sketch_ref[...], inverse_ref[...], ((1,), (1,)), HIGHEST)
    projected_ref[0] = dot(mine_ref[...], inverse_ref[...], ((1,), (1,)), HIGHEST) * (1.0 / total**0.5)


def factor(packed, mine, sketch, total):
    rows, rank = sketch.shape
    return pl.pallas_call(
        functools.partial(factor_kernel, total),
        in_specs=[WHOLE] * 3,
        out_specs=(WHOLE,) * 3,
        out_shape=(
            jax.ShapeDtypeStruct(sketch.shape, F32),
            jax.ShapeDtypeStruct((rank, rank), F32),
            jax.ShapeDtypeStruct((1,) + mine.shape, F32),
        ),
        scratch_shapes=[pltpu.VMEM((rank, rank), F32)],
        compiler_params=pltpu.CompilerParams(vmem_limit_bytes=LIMIT),
        cost_estimate=cost(50 * 2 * rows * rank * rank, rows * rank, rows * rank),
        name="factor",
    )(packed, mine, sketch)


def exchange(parts, axis):
    return lax.all_to_all(parts, axis, 0, 0)


def body(samples, start_basis):
    rows, columns = samples.shape
    rank = start_basis.shape[1]
    y, x, cores, n_col = (lax.axis_size(name) for name in ("y", "x", "core", "col"))
    total = rows * y * x * cores
    share, gram = columns // (y * x * cores), gram_rows(rank)

    local, samples = sketch_product(samples, start_basis)
    chunks = sum_and_copy(exchange(local.reshape(n_col, rows // n_col, rank), "col"))
    sketch = exchange(chunks, "col").reshape(rows, rank)

    own, other = products(samples, sketch, share)
    received = lax.ppermute(other, "core", [(0, 1), (1, 0)])
    parts = exchange(spread([own, received], share, x, gram), "x")
    parts = exchange(respread(parts, share, gram), "y")
    mine, half = finish(parts, share)
    packed = lax.all_gather(half, "core", axis=0, tiled=True)
    return factor(packed, mine, sketch, float(total))


def solution(mesh):
    split = jax.sharding.Mesh(mesh.devices.reshape(8, 4, 2, 8), ("y", "x", "core", "col"))
    row = ("y", "x", "core")
    in_specs = (P(row, "col"), P("col", None))
    out_specs = (P(row, None), P(), P("col", row, None))
    return jax.shard_map(body, mesh=split, in_specs=in_specs, out_specs=out_specs, check_vma=False)
```

```python
import functools

import jax
import jax.numpy as jnp
from jax import lax
from jax.experimental import pallas as pl
from jax.experimental.pallas import tpu as pltpu
from jax.sharding import PartitionSpec as P

F32, BF16 = jnp.float32, jnp.bfloat16
HIGHEST = lax.Precision.HIGHEST
WHOLE = pl.BlockSpec(memory_space=pltpu.VMEM)
SUBLANES = 8
LIMIT = 12 * 2**20


def halves(values):
    high = values.astype(BF16)
    return high, (values - high.astype(F32)).astype(BF16)


def dot(left, right, axes, precision=None):
    return lax.dot_general(
        left, right, (axes, ((), ())), precision=precision, preferred_element_type=F32
    )


def cost(flops, read, written):
    return pl.CostEstimate(flops=flops, bytes_accessed=4 * (read + written), transcendentals=0)


def split_dot(left, right_halves, axes):
    high, low = halves(left)
    both = dot(high, right_halves, axes) + dot(low, right_halves, axes)
    rank = right_halves.shape[1] // 2
    return both[:, :rank] + both[:, rank:]


def sketch_kernel(step, block, samples_ref, start_ref, local_ref, held_ref, start, sems):
    rows, columns = held_ref.shape
    rank = local_ref.shape[1]
    copies = []
    for i in range(columns // step):
        at = pl.ds(i * step, step)
        pair = (
            pltpu.make_async_copy(start_ref.at[at], start.at[at], sems.at[0, i]),
            pltpu.make_async_copy(samples_ref.at[:, at], held_ref.at[:, at], sems.at[1, i]),
        )
        for copy in pair:
            copy.start()
        copies.append(pair)
    for i, pair in enumerate(copies):
        for copy in pair:
            copy.wait()
        at = slice(i * step, (i + 1) * step)
        right = jnp.concatenate(halves(start[at]), axis=1)
        for first in range(0, rows, block):
            here = slice(first, first + block)
            left = jnp.concatenate(halves(held_ref[here, at]), axis=0)
            both = dot(left, right, ((1,), (0,)))
            both = both[:block] + both[block:]
            both = both[:, :rank] + both[:, rank:]
            local_ref[here] = both if i == 0 else local_ref[here] + both


def sketch_product(samples, start_basis, step=256, block=128):
    rows, columns = samples.shape
    rank = start_basis.shape[1]
    samples, start_basis = (
        pltpu.with_memory_space_constraint(values, pltpu.HBM) for values in (samples, start_basis)
    )
    return pl.pallas_call(
        functools.partial(sketch_kernel, step, block),
        in_specs=[pl.BlockSpec(memory_space=pltpu.HBM)] * 2,
        out_specs=(WHOLE, WHOLE),
        out_shape=(
            jax.ShapeDtypeStruct((rows, rank), F32),
            jax.ShapeDtypeStruct((rows, columns), F32),
        ),
        scratch_shapes=[
            pltpu.VMEM((columns, rank), F32),
            pltpu.SemaphoreType.DMA((2, columns // step)),
        ],
        compiler_params=pltpu.CompilerParams(vmem_limit_bytes=LIMIT),
        cost_estimate=cost(8 * rows * columns * rank, rows * columns, rows * rank),
        name="sketch_product",
    )(samples, start_basis)


def sum_kernel(parts_ref, out_ref):
    total = parts_ref[0]
    for i in range(1, parts_ref.shape[0]):
        total = total + parts_ref[i]
    for i in range(out_ref.shape[0]):
        out_ref[i] = total


def sum_and_copy(parts):
    return pl.pallas_call(
        sum_kernel,
        in_specs=[WHOLE],
        out_specs=WHOLE,
        out_shape=jax.ShapeDtypeStruct(parts.shape, F32),
        compiler_params=pltpu.CompilerParams(vmem_limit_bytes=LIMIT),
        cost_estimate=cost(parts.size, parts.size, parts.size),
        name="sum_and_copy",
    )(parts)


def products_kernel(step, share, samples_ref, sketch_ref, own_ref, other_ref, sketch_halves):
    core = lax.axis_index("core")
    rank = sketch_ref.shape[1]

    def give(at, for_first, for_second):
        here = slice(at, at + for_first.shape[0])
        own_ref[here] = jnp.where(core == 0, for_first, for_second)
        other_ref[here] = jnp.where(core == 0, for_second, for_first)

    sketch = sketch_ref[...]
    gram = dot(sketch, sketch, ((0,), (0,)), HIGHEST)
    tiles = [gram[at : at + SUBLANES] for at in range(0, rank, SUBLANES)]
    packed = packed_tiles(tiles)
    middle = len(packed) // 2 + 1
    first, second = packed[:middle], packed[middle:]
    second += [jnp.zeros_like(gram[:SUBLANES])] * (len(first) - len(second))
    for i, pair in enumerate(zip(first, second)):
        give(samples_ref.shape[1] // 2 + SUBLANES * i, *pair)

    high, low = halves(sketch)
    sketch_halves[:, :rank] = high
    sketch_halves[:, rank:] = low
    for at in range(0, samples_ref.shape[1], step):
        wide = split_dot(samples_ref[:, at : at + step], sketch_halves[...], ((0,), (0,)))
        for begin in range(0, step, 2 * share):
            pair = [wide[begin + share * i : begin + share * (i + 1)] for i in range(2)]
            give((at + begin) // 2, *pair)


def packed_tiles(tiles):
    count, size = len(tiles), tiles[0].shape[1]
    lane = lax.broadcasted_iota(jnp.int32, tiles[0].shape, 1)
    packed = [tiles[0]]
    for t in range(1, count // 2):
        start = SUBLANES * t
        packed.append(jnp.where(lane >= start, tiles[t], pltpu.roll(tiles[count - t], start, 1)))
    return packed + [tiles[count // 2]]


def unpacked_tiles(packed):
    count, size = 2 * (len(packed) - 1), packed[0].shape[1]
    tiles = list(packed) + [None] * (count - len(packed))
    for t in range(1, count // 2):
        tiles[count - t] = pltpu.roll(packed[t], size - SUBLANES * t, 1)
    upper = jnp.concatenate(tiles, axis=0)
    row = lax.broadcasted_iota(jnp.int32, upper.shape, 0)
    lane = lax.broadcasted_iota(jnp.int32, upper.shape, 1)
    whole = jnp.where(lane >= row // SUBLANES * SUBLANES, upper, upper.T)
    return [whole[at : at + SUBLANES] for at in range(0, size, SUBLANES)]


def gram_rows(rank):
    return SUBLANES * (rank // SUBLANES // 4 + 1)


def products(samples, sketch, share, step=256):
    rows, columns = samples.shape
    rank = sketch.shape[1]
    half = jax.ShapeDtypeStruct((columns // 2 + gram_rows(rank), rank), F32)
    return pl.pallas_call(
        functools.partial(products_kernel, step, share),
        in_specs=[WHOLE, WHOLE],
        out_specs=(WHOLE, WHOLE),
        out_shape=(half, half),
        scratch_shapes=[pltpu.VMEM((rows, 2 * rank), BF16)],
        compiler_params=pltpu.CompilerParams(vmem_limit_bytes=LIMIT),
        cost_estimate=cost(8 * rows * columns * rank, rows * columns, columns * rank),
        name="products",
    )(samples, sketch)


def added(refs, at, rows):
    total = refs[0][at : at + rows]
    for ref in refs[1:]:
        total = total + ref[at : at + rows]
    return total


def spread_kernel(share, inner, outer, gram, own_ref, others_ref, out_ref):
    rows = own_ref.shape[0]
    theirs = (1 - lax.axis_index("core")) * rows

    def total(at, count):
        there = pl.ds(pl.multiple_of(theirs + at, SUBLANES), count)
        return own_ref[at : at + count] + others_ref[there]

    last = total(outer * inner * share, gram)
    size = outer * share + gram
    for i in range(inner):
        for o in range(outer):
            here = size * i + share * o
            out_ref[here : here + share] = total((o * inner + i) * share, share)
        out_ref[size * (i + 1) - gram : size * (i + 1)] = last


def spread(own, others, share, inner, gram):
    rows, rank = own.shape
    outer = (rows - gram) // share // inner
    size = outer * share + gram
    out = pl.pallas_call(
        functools.partial(spread_kernel, share, inner, outer, gram),
        in_specs=[WHOLE] * 2,
        out_specs=WHOLE,
        out_shape=jax.ShapeDtypeStruct((inner * size, rank), F32),
        compiler_params=pltpu.CompilerParams(vmem_limit_bytes=LIMIT),
        cost_estimate=cost(rows * rank, rows * rank, inner * size * rank),
        name="spread",
    )(own, others)
    return out.reshape(inner, size, rank)


def respread_kernel(share, count, gram, parts_ref, out_ref):
    parts = [parts_ref.at[i] for i in range(parts_ref.shape[0])]
    last = added(parts, count * share, gram)
    for i in range(count):
        out_ref[i, :share] = added(parts, i * share, share)
        out_ref[i, share:] = last


def respread(parts, share, gram):
    count = (parts.shape[1] - gram) // share
    rank = parts.shape[2]
    return pl.pallas_call(
        functools.partial(respread_kernel, share, count, gram),
        in_specs=[WHOLE],
        out_specs=WHOLE,
        out_shape=jax.ShapeDtypeStruct((count, share + gram, rank), F32),
        compiler_params=pltpu.CompilerParams(vmem_limit_bytes=LIMIT),
        cost_estimate=cost(parts.size, parts.size, parts.size),
        name="respread",
    )(parts)


def finish_kernel(parts_ref, mine_ref, gram_ref):
    parts = [parts_ref.at[i] for i in range(parts_ref.shape[0])]
    share, gram = mine_ref.shape[0], gram_ref.shape[0]
    mine_ref[...] = added(parts, 0, share)
    gram_ref[...] = added(parts, share, gram)


def finish(parts, share):
    rows, rank = parts.shape[1:]
    return pl.pallas_call(
        finish_kernel,
        in_specs=[WHOLE],
        out_specs=(WHOLE, WHOLE),
        out_shape=(
            jax.ShapeDtypeStruct((share, rank), F32),
            jax.ShapeDtypeStruct((rows - share, rank), F32),
        ),
        compiler_params=pltpu.CompilerParams(vmem_limit_bytes=LIMIT),
        cost_estimate=cost(parts.size, parts.size, rows * rank),
        name="finish",
    )(parts)


def factor_kernel(
    total, packed_ref, mine_ref, sketch_ref, basis_ref, upper_ref, projected_ref, inverse_ref
):
    size = upper_ref.shape[0]
    count = size // SUBLANES
    lane = lax.broadcasted_iota(jnp.int32, (SUBLANES, size), 1)
    sub = lax.broadcasted_iota(jnp.int32, (SUBLANES, size), 0)
    down = lambda values, row: jnp.broadcast_to(values[row : row + 1, :], values.shape)
    across = lambda values, column: jnp.broadcast_to(values[:, column : column + 1], values.shape)
    packed = [packed_ref[SUBLANES * i : SUBLANES * (i + 1)] for i in range(count // 2 + 1)]
    tiles = [tile / total for tile in unpacked_tiles(packed)]
    columns = lambda t, j: [across(tiles[t], SUBLANES * j + k) for k in range(SUBLANES)]
    own, below = columns(0, 0), {1: columns(1, 0)}
    for j in range(count):
        base = SUBLANES * j
        here = slice(base, base + SUBLANES)
        inside = (lane >= base) & (lane < base + SUBLANES)
        near = range(j + 1, min(j + 1 + 4, count))
        for t in near[1:]:
            below[t] = columns(t, j)
        ahead = [columns(t, j + 1) for t in near[:2]]
        terms = [[None] * SUBLANES for t in near[:2]]
        panel = jnp.where(inside, jnp.where(lane - base == sub, 1.0, 0.0), tiles[j])
        for t in range(j + 1, count):
            tiles[t] = jnp.where(inside, 0.0, tiles[t])
        diagonal = jnp.ones_like(panel)
        for k in range(SUBLANES):
            later = range(k + 1, SUBLANES)
            pivot = down(own[k], k)
            reciprocal = 1.0 / pivot
            heads = {i: down(own[i], k) for i in later}
            diagonal = jnp.where(sub == k, pivot, diagonal)
            row = down(panel, k)
            factor = jnp.where(sub > k, own[k] * reciprocal, 0.0)
            for i in later:
                own[i] = own[i] - factor * heads[i]
            panel = panel - factor * row
            for t in near:
                factor = below[t][k] * reciprocal
                for i in later:
                    below[t][i] = below[t][i] - factor * heads[i]
                tiles[t] = tiles[t] - factor * row
                if t < j + 3:
                    for i in range(SUBLANES):
                        term = factor * down(below[j + 1][k], i)
                        known = terms[t - j - 1][i]
                        terms[t - j - 1][i] = term if known is None else known + term
        ahead = [[v - u for v, u in zip(*pair)] for pair in zip(ahead, terms)]
        owned = own
        if ahead:
            own, below = ahead[0], {j + 2: ahead[-1]}
        root = lax.rsqrt(diagonal)
        done = panel * root
        if near and near[-1] + 1 < count:
            first = done.astype(BF16).astype(F32)
            second = (done - first).astype(BF16).astype(F32)
            third = done - first - second
            left = jnp.concatenate([first, first, second, first, third, second], axis=0).astype(BF16)
            right = jnp.concatenate([first, second, first, third, first, second], axis=0).astype(BF16)
            update = dot(left, right, ((0,), (0,)))
            for t in range(near[-1] + 1, count):
                tiles[t] = tiles[t] - update[SUBLANES * t : SUBLANES * (t + 1)]
        block = jnp.zeros_like(panel)
        for k in range(SUBLANES):
            block = jnp.where(lane == base + k, owned[k] * root, block)
        block = jnp.where(lane - base >= sub, block, 0.0)
        upper_ref[here, :] = jnp.where(lane >= base + SUBLANES, done, block)
        inverse_ref[here, :] = jnp.where(lane < base + SUBLANES, done, 0.0)
    basis_ref[...] = dot(sketch_ref[...], inverse_ref[...], ((1,), (1,)), HIGHEST)
    projected_ref[0] = dot(mine_ref[...], inverse_ref[...], ((1,), (1,)), HIGHEST) * (1.0 / total**0.5)


def factor(packed, mine, sketch, total):
    rows, rank = sketch.shape
    return pl.pallas_call(
        functools.partial(factor_kernel, total),
        in_specs=[WHOLE] * 3,
        out_specs=(WHOLE,) * 3,
        out_shape=(
            jax.ShapeDtypeStruct(sketch.shape, F32),
            jax.ShapeDtypeStruct((rank, rank), F32),
            jax.ShapeDtypeStruct((1,) + mine.shape, F32),
        ),
        scratch_shapes=[pltpu.VMEM((rank, rank), F32)],
        compiler_params=pltpu.CompilerParams(vmem_limit_bytes=LIMIT),
        cost_estimate=cost(50 * 2 * rows * rank * rank, rows * rank, rows * rank),
        name="factor",
    )(packed, mine, sketch)


def exchange(parts, axis):
    return lax.all_to_all(parts, axis, 0, 0)


def body(samples, start_basis):
    rows, columns = samples.shape
    rank = start_basis.shape[1]
    y, x, cores, n_col = (lax.axis_size(name) for name in ("y", "x", "core", "col"))
    total = rows * y * x * cores
    share, gram = columns // (y * x * cores), gram_rows(rank)

    local, samples = sketch_product(samples, start_basis)
    chunks = sum_and_copy(exchange(local.reshape(n_col, rows // n_col, rank), "col"))
    sketch = exchange(chunks, "col").reshape(rows, rank)

    own, other = products(samples, sketch, share)
    others = lax.all_gather(other, "core", axis=0, tiled=True)
    parts = exchange(spread(own, others, share, x, gram), "x")
    parts = exchange(respread(parts, share, gram), "y")
    mine, half = finish(parts, share)
    packed = lax.all_gather(half, "core", axis=0, tiled=True)
    return factor(packed, mine, sketch, float(total))


def solution(mesh):
    split = jax.sharding.Mesh(mesh.devices.reshape(8, 4, 2, 8), ("y", "x", "core", "col"))
    row = ("y", "x", "core")
    in_specs = (P(row, "col"), P("col", None))
    out_specs = (P(row, None), P(), P("col", row, None))
    return jax.shard_map(body, mesh=split, in_specs=in_specs, out_specs=out_specs, check_vma=False)
```

```python
import functools

import jax
import jax.numpy as jnp
from jax import lax
from jax.experimental import pallas as pl
from jax.experimental.pallas import tpu as pltpu
from jax.sharding import PartitionSpec as P

F32, BF16 = jnp.float32, jnp.bfloat16
HIGHEST = lax.Precision.HIGHEST
WHOLE = pl.BlockSpec(memory_space=pltpu.VMEM)
SUBLANES = 8
LIMIT = 12 * 2**20


def halves(values):
    high = values.astype(BF16)
    return high, (values - high.astype(F32)).astype(BF16)


def thirds(values):
    high, rest = values.astype(BF16), values - values.astype(BF16).astype(F32)
    middle = rest.astype(BF16)
    return [high, middle, (rest - middle.astype(F32)).astype(BF16)]


def dot(left, right, axes, precision=None):
    return lax.dot_general(
        left, right, (axes, ((), ())), precision=precision, preferred_element_type=F32
    )


def cost(flops, read, written):
    return pl.CostEstimate(flops=flops, bytes_accessed=4 * (read + written), transcendentals=0)


def split_dot(left, right_halves, axes):
    high, low = halves(left)
    both = dot(high, right_halves, axes) + dot(low, right_halves, axes)
    rank = right_halves.shape[1] // 2
    return both[:, :rank] + both[:, rank:]


def sketch_kernel(step, block, samples_ref, start_ref, local_ref, held_ref, start, sems, start_sem):
    rows, columns = held_ref.shape
    rank = local_ref.shape[1]
    whole = pltpu.make_async_copy(start_ref, start, start_sem)
    whole.start()
    copies = []
    for i in range(columns // step):
        at = pl.ds(i * step, step)
        copies.append(pltpu.make_async_copy(samples_ref.at[:, at], held_ref.at[:, at], sems.at[i]))
        copies[-1].start()
    whole.wait()
    right = jnp.concatenate(halves(start[...]), axis=1)
    for i, copy in enumerate(copies):
        copy.wait()
        at = slice(i * step, (i + 1) * step)
        for first in range(0, rows, block):
            here = slice(first, first + block)
            left = jnp.concatenate(halves(held_ref[here, at]), axis=0)
            both = dot(left, right[at], ((1,), (0,)))
            both = both[:block] + both[block:]
            both = both[:, :rank] + both[:, rank:]
            local_ref[here] = both if i == 0 else local_ref[here] + both


def sketch_product(samples, start_basis, step=512, block=128):
    rows, columns = samples.shape
    rank = start_basis.shape[1]
    samples, start_basis = (
        pltpu.with_memory_space_constraint(values, pltpu.HBM) for values in (samples, start_basis)
    )
    return pl.pallas_call(
        functools.partial(sketch_kernel, step, block),
        in_specs=[pl.BlockSpec(memory_space=pltpu.HBM)] * 2,
        out_specs=(WHOLE, WHOLE),
        out_shape=(
            jax.ShapeDtypeStruct((rows, rank), F32),
            jax.ShapeDtypeStruct((rows, columns), F32),
        ),
        scratch_shapes=[
            pltpu.VMEM((columns, rank), F32),
            pltpu.SemaphoreType.DMA((columns // step,)),
            pltpu.SemaphoreType.DMA,
        ],
        compiler_params=pltpu.CompilerParams(vmem_limit_bytes=LIMIT),
        cost_estimate=cost(8 * rows * columns * rank, rows * columns, rows * rank),
        name="sketch_product",
    )(samples, start_basis)


def sum_kernel(parts_ref, out_ref):
    total = parts_ref[0]
    for i in range(1, parts_ref.shape[0]):
        total = total + parts_ref[i]
    for i in range(out_ref.shape[0]):
        out_ref[i] = total


def sum_and_copy(parts):
    return pl.pallas_call(
        sum_kernel,
        in_specs=[WHOLE],
        out_specs=WHOLE,
        out_shape=jax.ShapeDtypeStruct(parts.shape, F32),
        compiler_params=pltpu.CompilerParams(vmem_limit_bytes=LIMIT),
        cost_estimate=cost(parts.size, parts.size, parts.size),
        name="sum_and_copy",
    )(parts)


def products_kernel(step, share, samples_ref, sketch_ref, own_ref, other_ref, sketch_halves):
    core = lax.axis_index("core")
    rank = sketch_ref.shape[1]

    def give(at, for_first, for_second):
        here = slice(at, at + for_first.shape[0])
        own_ref[here] = jnp.where(core == 0, for_first, for_second)
        other_ref[here] = jnp.where(core == 0, for_second, for_first)

    sketch = sketch_ref[...]
    parts = thirds(sketch)
    both = dot(parts[0], jnp.concatenate(parts, axis=1), ((0,), (0,)))
    mixed = both[:, rank : 2 * rank] + both[:, 2 * rank :]
    gram = both[:, :rank] + dot(parts[1], parts[1], ((0,), (0,))) + (mixed + mixed.T)
    tiles = [gram[at : at + SUBLANES] for at in range(0, rank, SUBLANES)]
    packed = packed_tiles(tiles)
    middle = len(packed) // 2
    first, second = packed[:middle] + packed[-1:], packed[middle:]
    for i, pair in enumerate(zip(first, second)):
        give(samples_ref.shape[1] // 2 + SUBLANES * i, *pair)

    high, low = parts[:2]
    sketch_halves[:, :rank] = high
    sketch_halves[:, rank:] = low
    for at in range(0, samples_ref.shape[1], step):
        wide = split_dot(samples_ref[:, at : at + step], sketch_halves[...], ((0,), (0,)))
        for begin in range(0, step, 2 * share):
            pair = [wide[begin + share * i : begin + share * (i + 1)] for i in range(2)]
            give((at + begin) // 2, *pair)


def packed_tiles(tiles):
    count, size = len(tiles), tiles[0].shape[1]
    lane = lax.broadcasted_iota(jnp.int32, tiles[0].shape, 1)
    packed = [tiles[0]]
    for t in range(1, count // 2):
        start = SUBLANES * t
        packed.append(jnp.where(lane >= start, tiles[t], pltpu.roll(tiles[count - t], start, 1)))
    last = tiles[count // 2]
    lower = pltpu.roll(pltpu.roll(last, size // 2, 1), SUBLANES // 2, 0)
    return packed + [jnp.where(lane >= size // 2, last, lower)]


def unpacked_tiles(packed):
    count, size = 2 * (len(packed) - 1), packed[0].shape[1]
    sub = lax.broadcasted_iota(jnp.int32, packed[0].shape, 0)
    tiles = list(packed) + [None] * (count - len(packed))
    for t in range(1, count // 2):
        tiles[count - t] = pltpu.roll(packed[t], size - SUBLANES * t, 1)
    tiles[count // 2] = jnp.where(sub < SUBLANES // 2, packed[-1], pltpu.roll(packed[-1], size // 2, 1))
    upper = jnp.concatenate(tiles, axis=0)
    row = lax.broadcasted_iota(jnp.int32, upper.shape, 0)
    lane = lax.broadcasted_iota(jnp.int32, upper.shape, 1)
    whole = jnp.where(lane >= row // SUBLANES * SUBLANES, upper, upper.T)
    return [whole[at : at + SUBLANES] for at in range(0, size, SUBLANES)]


def gram_rows(rank):
    return rank // 4 + SUBLANES // 2


def products(samples, sketch, share, step=512):
    rows, columns = samples.shape
    rank = sketch.shape[1]
    half = jax.ShapeDtypeStruct((columns // 2 + gram_rows(rank) + SUBLANES // 2, rank), F32)
    return pl.pallas_call(
        functools.partial(products_kernel, step, share),
        in_specs=[WHOLE, WHOLE],
        out_specs=(WHOLE, WHOLE),
        out_shape=(half, half),
        scratch_shapes=[pltpu.VMEM((rows, 2 * rank), BF16)],
        compiler_params=pltpu.CompilerParams(vmem_limit_bytes=LIMIT),
        cost_estimate=cost(8 * rows * columns * rank, rows * columns, columns * rank),
        name="products",
    )(samples, sketch)


def added(refs, at, rows):
    total = refs[0][at : at + rows]
    for ref in refs[1:]:
        total = total + ref[at : at + rows]
    return total


def spread_kernel(share, inner, outer, gram, own_ref, others_ref, out_ref):
    theirs = (1 - lax.axis_index("core")) * own_ref.shape[0]

    def total(at, count):
        there = pl.ds(pl.multiple_of(theirs + at, SUBLANES), count)
        return own_ref[at : at + count] + others_ref[there]

    last = total(outer * inner * share, gram)
    size = outer * share + gram
    for i in range(inner):
        for o in range(outer):
            here = size * i + share * o
            out_ref[here : here + share] = total((o * inner + i) * share, share)
        out_ref[size * (i + 1) - gram : size * (i + 1)] = last


def spread(own, others, share, inner, gram):
    rows, rank = own.shape
    outer = (rows - gram) // share // inner
    size = outer * share + gram
    return pl.pallas_call(
        functools.partial(spread_kernel, share, inner, outer, gram),
        in_specs=[WHOLE] * 2,
        out_specs=WHOLE,
        out_shape=jax.ShapeDtypeStruct((inner * size, rank), F32),
        compiler_params=pltpu.CompilerParams(vmem_limit_bytes=LIMIT),
        cost_estimate=cost(rows * rank, rows * rank, inner * size * rank),
        name="spread",
    )(own, others)


def added(parts_ref, count, at, rows):
    size = parts_ref.shape[0] // count
    total = parts_ref[at : at + rows]
    for i in range(1, count):
        total = total + parts_ref[i * size + at : i * size + at + rows]
    return total


def respread_kernel(share, inner, outer, gram, parts_ref, out_ref):
    last = added(parts_ref, inner, outer * share, gram)
    for o in range(outer):
        here = (share + gram) * o
        out_ref[here : here + share] = added(parts_ref, inner, o * share, share)
        out_ref[here + share : here + share + gram] = last


def respread(parts, share, inner, outer, gram):
    rank = parts.shape[1]
    return pl.pallas_call(
        functools.partial(respread_kernel, share, inner, outer, gram),
        in_specs=[WHOLE],
        out_specs=WHOLE,
        out_shape=jax.ShapeDtypeStruct((outer * (share + gram), rank), F32),
        compiler_params=pltpu.CompilerParams(vmem_limit_bytes=LIMIT),
        cost_estimate=cost(parts.size, parts.size, parts.size),
        name="respread",
    )(parts)


def finish_kernel(outer, gram, parts_ref, mine_ref, gram_ref):
    share, whole = mine_ref.shape[0], gram // SUBLANES * SUBLANES
    mine_ref[...] = added(parts_ref, outer, 0, share)
    gram_ref[:whole] = added(parts_ref, outer, share, whole)
    last = added(parts_ref, outer, share + whole, gram - whole)
    gram_ref[whole:] = jnp.concatenate([last, last], axis=0)


def finish(parts, share, outer, gram):
    rank = parts.shape[1]
    return pl.pallas_call(
        functools.partial(finish_kernel, outer, gram),
        in_specs=[WHOLE],
        out_specs=(WHOLE, WHOLE),
        out_shape=(
            jax.ShapeDtypeStruct((share, rank), F32),
            jax.ShapeDtypeStruct((gram + SUBLANES // 2, rank), F32),
        ),
        compiler_params=pltpu.CompilerParams(vmem_limit_bytes=LIMIT),
        cost_estimate=cost(parts.size, parts.size, (share + gram) * rank),
        name="finish",
    )(parts)


def factor_kernel(
    total, packed_ref, mine_ref, sketch_ref, basis_ref, upper_ref, projected_ref, inverse_ref
):
    size = upper_ref.shape[0]
    count = size // SUBLANES
    lane = lax.broadcasted_iota(jnp.int32, (SUBLANES, size), 1)
    sub = lax.broadcasted_iota(jnp.int32, (SUBLANES, size), 0)
    down = lambda values, row: jnp.broadcast_to(values[row : row + 1, :], values.shape)
    across = lambda values, column: jnp.broadcast_to(values[:, column : column + 1], values.shape)
    middle = count // 4
    packed = [packed_ref[SUBLANES * i : SUBLANES * (i + 1)] for i in range(2 * (middle + 1))]
    packed = packed[:middle] + packed[middle + 1 :]
    tiles = [tile / total for tile in unpacked_tiles(packed)]
    columns = lambda t, j: [across(tiles[t], SUBLANES * j + k) for k in range(SUBLANES)]
    own, below = columns(0, 0), {1: columns(1, 0)}
    for j in range(count):
        base = SUBLANES * j
        here = slice(base, base + SUBLANES)
        inside = (lane >= base) & (lane < base + SUBLANES)
        near = range(j + 1, min(j + 1 + 4, count))
        for t in near[1:]:
            below[t] = columns(t, j)
        ahead = [columns(t, j + 1) for t in near[:2]]
        terms = [[None] * SUBLANES for t in near[:2]]
        panel = jnp.where(inside, jnp.where(lane - base == sub, 1.0, 0.0), tiles[j])
        for t in range(j + 1, count):
            tiles[t] = jnp.where(inside, 0.0, tiles[t])
        diagonal = jnp.ones_like(panel)
        for k in range(SUBLANES):
            later = range(k + 1, SUBLANES)
            pivot = down(own[k], k)
            reciprocal = 1.0 / pivot
            heads = {i: down(own[i], k) for i in later}
            diagonal = jnp.where(sub == k, pivot, diagonal)
            row = down(panel, k)
            factor = jnp.where(sub > k, own[k] * reciprocal, 0.0)
            for i in later:
                own[i] = own[i] - factor * heads[i]
            panel = panel - factor * row
            for t in near:
                factor = below[t][k] * reciprocal
                for i in later:
                    below[t][i] = below[t][i] - factor * heads[i]
                tiles[t] = tiles[t] - factor * row
                if t < j + 3:
                    for i in range(SUBLANES):
                        term = factor * down(below[j + 1][k], i)
                        known = terms[t - j - 1][i]
                        terms[t - j - 1][i] = term if known is None else known + term
        ahead = [[v - u for v, u in zip(*pair)] for pair in zip(ahead, terms)]
        owned = own
        if ahead:
            own, below = ahead[0], {j + 2: ahead[-1]}
        root = lax.rsqrt(diagonal)
        done = panel * root
        if near and near[-1] + 1 < count:
            first = done.astype(BF16).astype(F32)
            second = (done - first).astype(BF16).astype(F32)
            third = done - first - second
            left = jnp.concatenate([first, first, second, first, third, second], axis=0).astype(BF16)
            right = jnp.concatenate([first, second, first, third, first, second], axis=0).astype(BF16)
            update = dot(left, right, ((0,), (0,)))
            for t in range(near[-1] + 1, count):
                tiles[t] = tiles[t] - update[SUBLANES * t : SUBLANES * (t + 1)]
        block = jnp.zeros_like(panel)
        for k in range(SUBLANES):
            block = jnp.where(lane == base + k, owned[k] * root, block)
        block = jnp.where(lane - base >= sub, block, 0.0)
        upper_ref[here, :] = jnp.where(lane >= base + SUBLANES, done, block)
        inverse_ref[here, :] = jnp.where(lane < base + SUBLANES, done, 0.0)
    basis_ref[...] = dot(sketch_ref[...], inverse_ref[...], ((1,), (1,)), HIGHEST)
    projected_ref[0] = dot(mine_ref[...], inverse_ref[...], ((1,), (1,)), HIGHEST) * (1.0 / total**0.5)


def factor(packed, mine, sketch, total):
    rows, rank = sketch.shape
    return pl.pallas_call(
        functools.partial(factor_kernel, total),
        in_specs=[WHOLE] * 3,
        out_specs=(WHOLE,) * 3,
        out_shape=(
            jax.ShapeDtypeStruct(sketch.shape, F32),
            jax.ShapeDtypeStruct((rank, rank), F32),
            jax.ShapeDtypeStruct((1,) + mine.shape, F32),
        ),
        scratch_shapes=[pltpu.VMEM((rank, rank), F32)],
        compiler_params=pltpu.CompilerParams(vmem_limit_bytes=LIMIT),
        cost_estimate=cost(50 * 2 * rows * rank * rank, rows * rank, rows * rank),
        name="factor",
    )(packed, mine, sketch)


def exchange(parts, axis):
    return lax.all_to_all(parts, axis, 0, 0)


def body(samples, start_basis):
    rows, columns = samples.shape
    rank = start_basis.shape[1]
    y, x, cores, n_col = (lax.axis_size(name) for name in ("y", "x", "core", "col"))
    total = rows * y * x * cores
    share, gram = columns // (y * x * cores), gram_rows(rank)

    local, samples = sketch_product(samples, start_basis)
    chunks = sum_and_copy(exchange(local.reshape(n_col, rows // n_col, rank), "col"))
    sketch = exchange(chunks, "col").reshape(rows, rank)

    own, other = products(samples, sketch, share)
    others = lax.all_gather(other, "core", axis=0, tiled=True)
    trip = lambda parts, axis, n: exchange(parts.reshape(n, -1, 4, rank), axis).reshape(-1, rank)
    parts = trip(spread(own, others, share, x, gram), "x", x)
    parts = trip(respread(parts, share, x, y, gram), "y", y)
    mine, half = finish(parts, share, y, gram)
    packed = lax.all_gather(half, "core", axis=0, tiled=True)
    return factor(packed, mine, sketch, float(total))


def solution(mesh):
    split = jax.sharding.Mesh(mesh.devices.reshape(8, 4, 2, 8), ("y", "x", "core", "col"))
    row = ("y", "x", "core")
    in_specs = (P(row, "col"), P("col", None))
    out_specs = (P(row, None), P(), P("col", row, None))
    return jax.shard_map(body, mesh=split, in_specs=in_specs, out_specs=out_specs, check_vma=False)
```

```python
import functools

import jax
import jax.numpy as jnp
from jax import lax
from jax.experimental import pallas as pl
from jax.experimental.pallas import tpu as pltpu
from jax.sharding import PartitionSpec as P

F32, BF16 = jnp.float32, jnp.bfloat16
HIGHEST = lax.Precision.HIGHEST
WHOLE = pl.BlockSpec(memory_space=pltpu.VMEM)
SUBLANES = 8
LIMIT = 12 * 2**20


def halves(values):
    high = values.astype(BF16)
    return high, (values - high.astype(F32)).astype(BF16)


def thirds(values):
    high, rest = values.astype(BF16), values - values.astype(BF16).astype(F32)
    middle = rest.astype(BF16)
    return [high, middle, (rest - middle.astype(F32)).astype(BF16)]


def dot(left, right, axes, precision=None):
    return lax.dot_general(
        left, right, (axes, ((), ())), precision=precision, preferred_element_type=F32
    )


def cost(flops, read, written):
    return pl.CostEstimate(flops=flops, bytes_accessed=4 * (read + written), transcendentals=0)


def split_dot(left, right_halves, axes):
    high, low = halves(left)
    both = dot(high, right_halves, axes) + dot(low, right_halves, axes)
    rank = right_halves.shape[1] // 2
    return both[:, :rank] + both[:, rank:]


def sketch_kernel(step, block, samples_ref, start_ref, local_ref, held_ref, start, sems, start_sem):
    rows, columns = held_ref.shape
    rank = local_ref.shape[1]
    whole = pltpu.make_async_copy(start_ref, start, start_sem)
    whole.start()
    copies = []
    for i in range(columns // step):
        at = pl.ds(i * step, step)
        copies.append(pltpu.make_async_copy(samples_ref.at[:, at], held_ref.at[:, at], sems.at[i]))
        copies[-1].start()
    whole.wait()
    right = jnp.concatenate(halves(start[...]), axis=1)
    for i, copy in enumerate(copies):
        copy.wait()
        at = slice(i * step, (i + 1) * step)
        for first in range(0, rows, block):
            here = slice(first, first + block)
            left = jnp.concatenate(halves(held_ref[here, at]), axis=0)
            both = dot(left, right[at], ((1,), (0,)))
            both = both[:block] + both[block:]
            both = both[:, :rank] + both[:, rank:]
            local_ref[here] = both if i == 0 else local_ref[here] + both


def sketch_product(samples, start_basis, step=512, block=128):
    rows, columns = samples.shape
    rank = start_basis.shape[1]
    samples, start_basis = (
        pltpu.with_memory_space_constraint(values, pltpu.HBM) for values in (samples, start_basis)
    )
    return pl.pallas_call(
        functools.partial(sketch_kernel, step, block),
        in_specs=[pl.BlockSpec(memory_space=pltpu.HBM)] * 2,
        out_specs=(WHOLE, WHOLE),
        out_shape=(
            jax.ShapeDtypeStruct((rows, rank), F32),
            jax.ShapeDtypeStruct((rows, columns), F32),
        ),
        scratch_shapes=[
            pltpu.VMEM((columns, rank), F32),
            pltpu.SemaphoreType.DMA((columns // step,)),
            pltpu.SemaphoreType.DMA,
        ],
        compiler_params=pltpu.CompilerParams(vmem_limit_bytes=LIMIT),
        cost_estimate=cost(8 * rows * columns * rank, rows * columns, rows * rank),
        name="sketch_product",
    )(samples, start_basis)


def sum_kernel(parts_ref, out_ref):
    total = parts_ref[0]
    for i in range(1, parts_ref.shape[0]):
        total = total + parts_ref[i]
    for i in range(out_ref.shape[0]):
        out_ref[i] = total


def sum_and_copy(parts):
    return pl.pallas_call(
        sum_kernel,
        in_specs=[WHOLE],
        out_specs=WHOLE,
        out_shape=jax.ShapeDtypeStruct(parts.shape, F32),
        compiler_params=pltpu.CompilerParams(vmem_limit_bytes=LIMIT),
        cost_estimate=cost(parts.size, parts.size, parts.size),
        name="sum_and_copy",
    )(parts)


def products_kernel(step, share, samples_ref, sketch_ref, own_ref, other_ref, sketch_halves):
    core = lax.axis_index("core")
    rank = sketch_ref.shape[1]

    def give(at, for_first, for_second):
        here = slice(at, at + for_first.shape[0])
        own_ref[here] = jnp.where(core == 0, for_first, for_second)
        other_ref[here] = jnp.where(core == 0, for_second, for_first)

    sketch = sketch_ref[...]
    parts = thirds(sketch)
    both = dot(parts[0], jnp.concatenate(parts, axis=1), ((0,), (0,)))
    mixed = both[:, rank : 2 * rank] + both[:, 2 * rank :]
    gram = both[:, :rank] + dot(parts[1], parts[1], ((0,), (0,))) + (mixed + mixed.T)
    tiles = [gram[at : at + SUBLANES] for at in range(0, rank, SUBLANES)]
    packed = packed_tiles(tiles)
    middle = len(packed) // 2
    first, second = packed[:middle] + packed[-1:], packed[middle:]
    for i, pair in enumerate(zip(first, second)):
        give(samples_ref.shape[1] // 2 + SUBLANES * i, *pair)

    high, low = parts[:2]
    sketch_halves[:, :rank] = high
    sketch_halves[:, rank:] = low
    for at in range(0, samples_ref.shape[1], step):
        wide = split_dot(samples_ref[:, at : at + step], sketch_halves[...], ((0,), (0,)))
        for begin in range(0, step, 2 * share):
            pair = [wide[begin + share * i : begin + share * (i + 1)] for i in range(2)]
            give((at + begin) // 2, *pair)


def packed_tiles(tiles):
    count, size = len(tiles), tiles[0].shape[1]
    lane = lax.broadcasted_iota(jnp.int32, tiles[0].shape, 1)
    packed = [tiles[0]]
    for t in range(1, count // 2):
        start = SUBLANES * t
        packed.append(jnp.where(lane >= start, tiles[t], pltpu.roll(tiles[count - t], start, 1)))
    last = tiles[count // 2]
    lower = pltpu.roll(pltpu.roll(last, size // 2, 1), SUBLANES // 2, 0)
    return packed + [jnp.where(lane >= size // 2, last, lower)]


def unpacked_tiles(packed):
    count, size = 2 * (len(packed) - 1), packed[0].shape[1]
    sub = lax.broadcasted_iota(jnp.int32, packed[0].shape, 0)
    tiles = list(packed) + [None] * (count - len(packed))
    for t in range(1, count // 2):
        tiles[count - t] = pltpu.roll(packed[t], size - SUBLANES * t, 1)
    tiles[count // 2] = jnp.where(sub < SUBLANES // 2, packed[-1], pltpu.roll(packed[-1], size // 2, 1))
    upper = jnp.concatenate(tiles, axis=0)
    row = lax.broadcasted_iota(jnp.int32, upper.shape, 0)
    lane = lax.broadcasted_iota(jnp.int32, upper.shape, 1)
    whole = jnp.where(lane >= row // SUBLANES * SUBLANES, upper, upper.T)
    return [whole[at : at + SUBLANES] for at in range(0, size, SUBLANES)]


def gram_rows(rank):
    return rank // 4 + SUBLANES // 2


def products(samples, sketch, share, step=512):
    rows, columns = samples.shape
    rank = sketch.shape[1]
    half = jax.ShapeDtypeStruct((columns // 2 + gram_rows(rank) + SUBLANES // 2, rank), F32)
    return pl.pallas_call(
        functools.partial(products_kernel, step, share),
        in_specs=[WHOLE, WHOLE],
        out_specs=(WHOLE, WHOLE),
        out_shape=(half, half),
        scratch_shapes=[pltpu.VMEM((rows, 2 * rank), BF16)],
        compiler_params=pltpu.CompilerParams(vmem_limit_bytes=LIMIT),
        cost_estimate=cost(8 * rows * columns * rank, rows * columns, columns * rank),
        name="products",
    )(samples, sketch)


def added(refs, at, rows):
    total = refs[0][at : at + rows]
    for ref in refs[1:]:
        total = total + ref[at : at + rows]
    return total


def spread_kernel(share, inner, outer, gram, own_ref, others_ref, out_ref):
    theirs = (1 - lax.axis_index("core")) * own_ref.shape[0]

    def total(at, count):
        there = pl.ds(pl.multiple_of(theirs + at, SUBLANES), count)
        return own_ref[at : at + count] + others_ref[there]

    last = total(outer * inner * share, gram)
    size = outer * share + gram
    for i in range(inner):
        for o in range(outer):
            here = size * i + share * o
            out_ref[here : here + share] = total((o * inner + i) * share, share)
        out_ref[size * (i + 1) - gram : size * (i + 1)] = last


def spread(own, others, share, inner, gram):
    rows, rank = own.shape
    outer = (rows - gram) // share // inner
    size = outer * share + gram
    return pl.pallas_call(
        functools.partial(spread_kernel, share, inner, outer, gram),
        in_specs=[WHOLE] * 2,
        out_specs=WHOLE,
        out_shape=jax.ShapeDtypeStruct((inner * size, rank), F32),
        compiler_params=pltpu.CompilerParams(vmem_limit_bytes=LIMIT),
        cost_estimate=cost(rows * rank, rows * rank, inner * size * rank),
        name="spread",
    )(own, others)


def added(parts_ref, count, at, rows):
    size = parts_ref.shape[0] // count
    total = parts_ref[at : at + rows]
    for i in range(1, count):
        total = total + parts_ref[i * size + at : i * size + at + rows]
    return total


def respread_kernel(share, inner, outer, gram, parts_ref, out_ref):
    last = added(parts_ref, inner, outer * share, gram)
    for o in range(outer):
        here = (share + gram) * o
        out_ref[here : here + share] = added(parts_ref, inner, o * share, share)
        out_ref[here + share : here + share + gram] = last


def respread(parts, share, inner, outer, gram):
    rank = parts.shape[1]
    return pl.pallas_call(
        functools.partial(respread_kernel, share, inner, outer, gram),
        in_specs=[WHOLE],
        out_specs=WHOLE,
        out_shape=jax.ShapeDtypeStruct((outer * (share + gram), rank), F32),
        compiler_params=pltpu.CompilerParams(vmem_limit_bytes=LIMIT),
        cost_estimate=cost(parts.size, parts.size, parts.size),
        name="respread",
    )(parts)


def finish_kernel(outer, gram, parts_ref, mine_ref, gram_ref):
    share, whole = mine_ref.shape[0], gram // SUBLANES * SUBLANES
    mine_ref[...] = added(parts_ref, outer, 0, share)
    gram_ref[:whole] = added(parts_ref, outer, share, whole)
    last = added(parts_ref, outer, share + whole, gram - whole)
    gram_ref[whole:] = jnp.concatenate([last, last], axis=0)


def finish(parts, share, outer, gram):
    rank = parts.shape[1]
    return pl.pallas_call(
        functools.partial(finish_kernel, outer, gram),
        in_specs=[WHOLE],
        out_specs=(WHOLE, WHOLE),
        out_shape=(
            jax.ShapeDtypeStruct((share, rank), F32),
            jax.ShapeDtypeStruct((gram + SUBLANES // 2, rank), F32),
        ),
        compiler_params=pltpu.CompilerParams(vmem_limit_bytes=LIMIT),
        cost_estimate=cost(parts.size, parts.size, (share + gram) * rank),
        name="finish",
    )(parts)


def factor_kernel(
    total, packed_ref, mine_ref, sketch_ref, basis_ref, upper_ref, projected_ref, inverse_ref
):
    size = upper_ref.shape[0]
    count = size // SUBLANES
    lane = lax.broadcasted_iota(jnp.int32, (SUBLANES, size), 1)
    sub = lax.broadcasted_iota(jnp.int32, (SUBLANES, size), 0)
    down = lambda values, row: jnp.broadcast_to(values[row : row + 1, :], values.shape)
    across = lambda values, column: jnp.broadcast_to(values[:, column : column + 1], values.shape)
    middle = count // 4
    packed = [packed_ref[SUBLANES * i : SUBLANES * (i + 1)] for i in range(2 * (middle + 1))]
    packed = packed[:middle] + packed[middle + 1 :]
    tiles = [tile / total for tile in unpacked_tiles(packed)]
    columns = lambda t, j: [across(tiles[t], SUBLANES * j + k) for k in range(SUBLANES)]
    own, below = columns(0, 0), {1: columns(1, 0)}
    for j in range(count):
        base = SUBLANES * j
        here = slice(base, base + SUBLANES)
        inside = (lane >= base) & (lane < base + SUBLANES)
        near = range(j + 1, min(j + 1 + 3, count))
        for t in near[1:]:
            below[t] = columns(t, j)
        ahead = [columns(t, j + 1) for t in near[:2]]
        terms = [[None] * SUBLANES for t in near[:2]]
        panel = jnp.where(inside, jnp.where(lane - base == sub, 1.0, 0.0), tiles[j])
        for t in range(j + 1, count):
            tiles[t] = jnp.where(inside, 0.0, tiles[t])
        diagonal = jnp.ones_like(panel)
        for k in range(SUBLANES):
            later = range(k + 1, SUBLANES)
            pivot = down(own[k], k)
            reciprocal = 1.0 / pivot
            heads = {i: down(own[i], k) for i in later}
            diagonal = jnp.where(sub == k, pivot, diagonal)
            row = down(panel, k)
            factor = jnp.where(sub > k, own[k] * reciprocal, 0.0)
            for i in later:
                own[i] = own[i] - factor * heads[i]
            panel = panel - factor * row
            for t in near:
                factor = below[t][k] * reciprocal
                for i in later:
                    below[t][i] = below[t][i] - factor * heads[i]
                tiles[t] = tiles[t] - factor * row
                if t < j + 3:
                    for i in range(SUBLANES):
                        term = factor * down(below[j + 1][k], i)
                        known = terms[t - j - 1][i]
                        terms[t - j - 1][i] = term if known is None else known + term
        ahead = [[v - u for v, u in zip(*pair)] for pair in zip(ahead, terms)]
        owned = own
        if ahead:
            own, below = ahead[0], {j + 2: ahead[-1]}
        root = lax.rsqrt(diagonal)
        done = panel * root
        if near and near[-1] + 1 < count:
            first = done.astype(BF16).astype(F32)
            second = (done - first).astype(BF16).astype(F32)
            third = done - first - second
            left = jnp.concatenate([first, first, second, first, third, second], axis=0).astype(BF16)
            right = jnp.concatenate([first, second, first, third, first, second], axis=0).astype(BF16)
            update = dot(left, right, ((0,), (0,)))
            for t in range(near[-1] + 1, count):
                tiles[t] = tiles[t] - update[SUBLANES * t : SUBLANES * (t + 1)]
        block = jnp.zeros_like(panel)
        for k in range(SUBLANES):
            block = jnp.where(lane == base + k, owned[k] * root, block)
        block = jnp.where(lane - base >= sub, block, 0.0)
        upper_ref[here, :] = jnp.where(lane >= base + SUBLANES, done, block)
        inverse_ref[here, :] = jnp.where(lane < base + SUBLANES, done, 0.0)
    basis_ref[...] = dot(sketch_ref[...], inverse_ref[...], ((1,), (1,)), HIGHEST)
    projected_ref[0] = dot(mine_ref[...], inverse_ref[...], ((1,), (1,)), HIGHEST) * (1.0 / total**0.5)


def factor(packed, mine, sketch, total):
    rows, rank = sketch.shape
    return pl.pallas_call(
        functools.partial(factor_kernel, total),
        in_specs=[WHOLE] * 3,
        out_specs=(WHOLE,) * 3,
        out_shape=(
            jax.ShapeDtypeStruct(sketch.shape, F32),
            jax.ShapeDtypeStruct((rank, rank), F32),
            jax.ShapeDtypeStruct((1,) + mine.shape, F32),
        ),
        scratch_shapes=[pltpu.VMEM((rank, rank), F32)],
        compiler_params=pltpu.CompilerParams(vmem_limit_bytes=LIMIT),
        cost_estimate=cost(50 * 2 * rows * rank * rank, rows * rank, rows * rank),
        name="factor",
    )(packed, mine, sketch)


def exchange(parts, axis):
    return lax.all_to_all(parts, axis, 0, 0)


def body(samples, start_basis):
    rows, columns = samples.shape
    rank = start_basis.shape[1]
    y, x, cores, n_col = (lax.axis_size(name) for name in ("y", "x", "core", "col"))
    total = rows * y * x * cores
    share, gram = columns // (y * x * cores), gram_rows(rank)

    local, samples = sketch_product(samples, start_basis)
    chunks = sum_and_copy(exchange(local.reshape(n_col, rows // n_col, rank), "col"))
    sketch = exchange(chunks, "col").reshape(rows, rank)

    own, other = products(samples, sketch, share)
    others = lax.all_gather(other, "core", axis=0, tiled=True)
    trip = lambda parts, axis, n: exchange(parts.reshape(n, -1, 4, rank), axis).reshape(-1, rank)
    parts = trip(spread(own, others, share, x, gram), "x", x)
    parts = trip(respread(parts, share, x, y, gram), "y", y)
    mine, half = finish(parts, share, y, gram)
    packed = lax.all_gather(half, "core", axis=0, tiled=True)
    return factor(packed, mine, sketch, float(total))


def solution(mesh):
    split = jax.sharding.Mesh(mesh.devices.reshape(8, 4, 2, 8), ("y", "x", "core", "col"))
    row = ("y", "x", "core")
    in_specs = (P(row, "col"), P("col", None))
    out_specs = (P(row, None), P(), P("col", row, None))
    return jax.shard_map(body, mesh=split, in_specs=in_specs, out_specs=out_specs, check_vma=False)
```

```python
import functools

import jax
import jax.numpy as jnp
from jax import lax
from jax.experimental import pallas as pl
from jax.experimental.pallas import tpu as pltpu
from jax.sharding import PartitionSpec as P

F32, BF16 = jnp.float32, jnp.bfloat16
HIGHEST = lax.Precision.HIGHEST
WHOLE = pl.BlockSpec(memory_space=pltpu.VMEM)
SUBLANES = 8
LIMIT = 12 * 2**20


def halves(values):
    high = values.astype(BF16)
    return high, (values - high.astype(F32)).astype(BF16)


def thirds(values):
    high, rest = values.astype(BF16), values - values.astype(BF16).astype(F32)
    middle = rest.astype(BF16)
    return [high, middle, (rest - middle.astype(F32)).astype(BF16)]


def dot(left, right, axes, precision=None):
    return lax.dot_general(
        left, right, (axes, ((), ())), precision=precision, preferred_element_type=F32
    )


def cost(flops, read, written):
    return pl.CostEstimate(flops=flops, bytes_accessed=4 * (read + written), transcendentals=0)


def split_dot(left, right_halves, axes):
    high, low = halves(left)
    both = dot(high, right_halves, axes) + dot(low, right_halves, axes)
    rank = right_halves.shape[1] // 2
    return both[:, :rank] + both[:, rank:]


def sketch_kernel(step, block, samples_ref, start_ref, local_ref, held_ref, start, sems, start_sem):
    rows, columns = held_ref.shape
    rank = local_ref.shape[1]
    whole = pltpu.make_async_copy(start_ref, start, start_sem)
    whole.start()
    copies = []
    for i in range(columns // step):
        at = pl.ds(i * step, step)
        copies.append(pltpu.make_async_copy(samples_ref.at[:, at], held_ref.at[:, at], sems.at[i]))
        copies[-1].start()
    whole.wait()
    right = jnp.concatenate(halves(start[...]), axis=1)
    for i, copy in enumerate(copies):
        copy.wait()
        at = slice(i * step, (i + 1) * step)
        for first in range(0, rows, block):
            here = slice(first, first + block)
            left = jnp.concatenate(halves(held_ref[here, at]), axis=0)
            both = dot(left, right[at], ((1,), (0,)))
            both = both[:block] + both[block:]
            both = both[:, :rank] + both[:, rank:]
            local_ref[here] = both if i == 0 else local_ref[here] + both


def sketch_product(samples, start_basis, step=512, block=128):
    rows, columns = samples.shape
    rank = start_basis.shape[1]
    samples, start_basis = (
        pltpu.with_memory_space_constraint(values, pltpu.HBM) for values in (samples, start_basis)
    )
    return pl.pallas_call(
        functools.partial(sketch_kernel, step, block),
        in_specs=[pl.BlockSpec(memory_space=pltpu.HBM)] * 2,
        out_specs=(WHOLE, WHOLE),
        out_shape=(
            jax.ShapeDtypeStruct((rows, rank), F32),
            jax.ShapeDtypeStruct((rows, columns), F32),
        ),
        scratch_shapes=[
            pltpu.VMEM((columns, rank), F32),
            pltpu.SemaphoreType.DMA((columns // step,)),
            pltpu.SemaphoreType.DMA,
        ],
        compiler_params=pltpu.CompilerParams(vmem_limit_bytes=LIMIT),
        cost_estimate=cost(8 * rows * columns * rank, rows * columns, rows * rank),
        name="sketch_product",
    )(samples, start_basis)


def sum_kernel(parts_ref, out_ref):
    total = parts_ref[0]
    for i in range(1, parts_ref.shape[0]):
        total = total + parts_ref[i]
    for i in range(out_ref.shape[0]):
        out_ref[i] = total


def sum_and_copy(parts):
    return pl.pallas_call(
        sum_kernel,
        in_specs=[WHOLE],
        out_specs=WHOLE,
        out_shape=jax.ShapeDtypeStruct(parts.shape, F32),
        compiler_params=pltpu.CompilerParams(vmem_limit_bytes=LIMIT),
        cost_estimate=cost(parts.size, parts.size, parts.size),
        name="sum_and_copy",
    )(parts)


def products_kernel(step, share, samples_ref, sketch_ref, own_ref, other_ref, sketch_halves):
    core = lax.axis_index("core")
    rank = sketch_ref.shape[1]

    def give(at, for_first, for_second):
        here = slice(at, at + for_first.shape[0])
        own_ref[here] = jnp.where(core == 0, for_first, for_second)
        other_ref[here] = jnp.where(core == 0, for_second, for_first)

    sketch = sketch_ref[...]
    parts = thirds(sketch)
    both = dot(parts[0], jnp.concatenate(parts, axis=1), ((0,), (0,)))
    mixed = both[:, rank : 2 * rank] + both[:, 2 * rank :]
    gram = both[:, :rank] + dot(parts[1], parts[1], ((0,), (0,))) + (mixed + mixed.T)
    tiles = [gram[at : at + SUBLANES] for at in range(0, rank, SUBLANES)]
    packed = packed_tiles(tiles)
    middle = len(packed) // 2
    first, second = packed[:middle] + packed[-1:], packed[middle:]
    for i, pair in enumerate(zip(first, second)):
        give(samples_ref.shape[1] // 2 + SUBLANES * i, *pair)

    high, low = parts[:2]
    sketch_halves[:, :rank] = high
    sketch_halves[:, rank:] = low
    for at in range(0, samples_ref.shape[1], step):
        wide = split_dot(samples_ref[:, at : at + step], sketch_halves[...], ((0,), (0,)))
        for begin in range(0, step, 2 * share):
            pair = [wide[begin + share * i : begin + share * (i + 1)] for i in range(2)]
            give((at + begin) // 2, *pair)


def packed_tiles(tiles):
    count, size = len(tiles), tiles[0].shape[1]
    lane = lax.broadcasted_iota(jnp.int32, tiles[0].shape, 1)
    packed = [tiles[0]]
    for t in range(1, count // 2):
        start = SUBLANES * t
        packed.append(jnp.where(lane >= start, tiles[t], pltpu.roll(tiles[count - t], start, 1)))
    last = tiles[count // 2]
    lower = pltpu.roll(pltpu.roll(last, size // 2, 1), SUBLANES // 2, 0)
    return packed + [jnp.where(lane >= size // 2, last, lower)]


def unpacked_tiles(packed):
    count, size = 2 * (len(packed) - 1), packed[0].shape[1]
    sub = lax.broadcasted_iota(jnp.int32, packed[0].shape, 0)
    tiles = list(packed) + [None] * (count - len(packed))
    for t in range(1, count // 2):
        tiles[count - t] = pltpu.roll(packed[t], size - SUBLANES * t, 1)
    tiles[count // 2] = jnp.where(sub < SUBLANES // 2, packed[-1], pltpu.roll(packed[-1], size // 2, 1))
    upper = jnp.concatenate(tiles, axis=0)
    row = lax.broadcasted_iota(jnp.int32, upper.shape, 0)
    lane = lax.broadcasted_iota(jnp.int32, upper.shape, 1)
    whole = jnp.where(lane >= row // SUBLANES * SUBLANES, upper, upper.T)
    return [whole[at : at + SUBLANES] for at in range(0, size, SUBLANES)]


def gram_rows(rank):
    return rank // 4 + SUBLANES // 2


def products(samples, sketch, share, step=512):
    rows, columns = samples.shape
    rank = sketch.shape[1]
    half = jax.ShapeDtypeStruct((columns // 2 + gram_rows(rank) + SUBLANES // 2, rank), F32)
    return pl.pallas_call(
        functools.partial(products_kernel, step, share),
        in_specs=[WHOLE, WHOLE],
        out_specs=(WHOLE, WHOLE),
        out_shape=(half, half),
        scratch_shapes=[pltpu.VMEM((rows, 2 * rank), BF16)],
        compiler_params=pltpu.CompilerParams(vmem_limit_bytes=LIMIT),
        cost_estimate=cost(8 * rows * columns * rank, rows * columns, columns * rank),
        name="products",
    )(samples, sketch)


def added(refs, at, rows):
    total = refs[0][at : at + rows]
    for ref in refs[1:]:
        total = total + ref[at : at + rows]
    return total


def spread_kernel(share, inner, outer, gram, own_ref, others_ref, out_ref):
    theirs = (1 - lax.axis_index("core")) * own_ref.shape[0]

    def total(at, count):
        there = pl.ds(pl.multiple_of(theirs + at, SUBLANES), count)
        return own_ref[at : at + count] + others_ref[there]

    last = total(outer * inner * share, gram)
    size = outer * share + gram
    for i in range(inner):
        for o in range(outer):
            here = size * i + share * o
            out_ref[here : here + share] = total((o * inner + i) * share, share)
        out_ref[size * (i + 1) - gram : size * (i + 1)] = last


def spread(own, others, share, inner, gram):
    rows, rank = own.shape
    outer = (rows - gram) // share // inner
    size = outer * share + gram
    return pl.pallas_call(
        functools.partial(spread_kernel, share, inner, outer, gram),
        in_specs=[WHOLE] * 2,
        out_specs=WHOLE,
        out_shape=jax.ShapeDtypeStruct((inner * size, rank), F32),
        compiler_params=pltpu.CompilerParams(vmem_limit_bytes=LIMIT),
        cost_estimate=cost(rows * rank, rows * rank, inner * size * rank),
        name="spread",
    )(own, others)


def added(parts_ref, count, at, rows):
    size = parts_ref.shape[0] // count
    total = parts_ref[at : at + rows]
    for i in range(1, count):
        total = total + parts_ref[i * size + at : i * size + at + rows]
    return total


def respread_kernel(share, inner, outer, gram, parts_ref, out_ref):
    last = added(parts_ref, inner, outer * share, gram)
    for o in range(outer):
        here = (share + gram) * o
        out_ref[here : here + share] = added(parts_ref, inner, o * share, share)
        out_ref[here + share : here + share + gram] = last


def respread(parts, share, inner, outer, gram):
    rank = parts.shape[1]
    return pl.pallas_call(
        functools.partial(respread_kernel, share, inner, outer, gram),
        in_specs=[WHOLE],
        out_specs=WHOLE,
        out_shape=jax.ShapeDtypeStruct((outer * (share + gram), rank), F32),
        compiler_params=pltpu.CompilerParams(vmem_limit_bytes=LIMIT),
        cost_estimate=cost(parts.size, parts.size, parts.size),
        name="respread",
    )(parts)


def finish_kernel(outer, gram, parts_ref, mine_ref, gram_ref):
    share, whole = mine_ref.shape[0], gram // SUBLANES * SUBLANES
    mine_ref[...] = added(parts_ref, outer, 0, share)
    gram_ref[:whole] = added(parts_ref, outer, share, whole)
    last = added(parts_ref, outer, share + whole, gram - whole)
    gram_ref[whole:] = jnp.concatenate([last, last], axis=0)


def finish(parts, share, outer, gram):
    rank = parts.shape[1]
    return pl.pallas_call(
        functools.partial(finish_kernel, outer, gram),
        in_specs=[WHOLE],
        out_specs=(WHOLE, WHOLE),
        out_shape=(
            jax.ShapeDtypeStruct((share, rank), F32),
            jax.ShapeDtypeStruct((gram + SUBLANES // 2, rank), F32),
        ),
        compiler_params=pltpu.CompilerParams(vmem_limit_bytes=LIMIT),
        cost_estimate=cost(parts.size, parts.size, (share + gram) * rank),
        name="finish",
    )(parts)


def factor_kernel(
    total, packed_ref, mine_ref, sketch_ref, basis_ref, upper_ref, projected_ref, inverse_ref, pieces_ref
):
    size = upper_ref.shape[0]
    count = size // SUBLANES
    lane = lax.broadcasted_iota(jnp.int32, (SUBLANES, size), 1)
    sub = lax.broadcasted_iota(jnp.int32, (SUBLANES, size), 0)
    down = lambda values, row: jnp.broadcast_to(values[row : row + 1, :], values.shape)
    across = lambda values, column: jnp.broadcast_to(values[:, column : column + 1], values.shape)
    middle = count // 4
    packed = [packed_ref[SUBLANES * i : SUBLANES * (i + 1)] for i in range(2 * (middle + 1))]
    packed = packed[:middle] + packed[middle + 1 :]
    tiles = [tile / total for tile in unpacked_tiles(packed)]
    first, second, third = thirds(sketch_ref[...])
    pieces_ref[...] = jnp.concatenate([second, first, third], axis=1)
    columns = lambda t, j: [across(tiles[t], SUBLANES * j + k) for k in range(SUBLANES)]
    own, below = columns(0, 0), {1: columns(1, 0)}
    for j in range(count):
        base = SUBLANES * j
        here = slice(base, base + SUBLANES)
        inside = (lane >= base) & (lane < base + SUBLANES)
        near = range(j + 1, min(j + 1 + 3, count))
        for t in near[1:]:
            below[t] = columns(t, j)
        ahead = [columns(t, j + 1) for t in near[:2]]
        terms = [[None] * SUBLANES for t in near[:2]]
        panel = jnp.where(inside, jnp.where(lane - base == sub, 1.0, 0.0), tiles[j])
        for t in range(j + 1, count):
            tiles[t] = jnp.where(inside, 0.0, tiles[t])
        diagonal = jnp.ones_like(panel)
        for k in range(SUBLANES):
            later = range(k + 1, SUBLANES)
            pivot = down(own[k], k)
            reciprocal = 1.0 / pivot
            heads = {i: down(own[i], k) for i in later}
            diagonal = jnp.where(sub == k, pivot, diagonal)
            row = down(panel, k)
            factor = jnp.where(sub > k, own[k] * reciprocal, 0.0)
            for i in later:
                own[i] = own[i] - factor * heads[i]
            panel = panel - factor * row
            for t in near:
                factor = below[t][k] * reciprocal
                for i in later:
                    below[t][i] = below[t][i] - factor * heads[i]
                tiles[t] = tiles[t] - factor * row
                if t < j + 3:
                    for i in range(SUBLANES):
                        term = factor * down(below[j + 1][k], i)
                        known = terms[t - j - 1][i]
                        terms[t - j - 1][i] = term if known is None else known + term
        ahead = [[v - u for v, u in zip(*pair)] for pair in zip(ahead, terms)]
        owned = own
        if ahead:
            own, below = ahead[0], {j + 2: ahead[-1]}
        root = lax.rsqrt(diagonal)
        done = panel * root
        if near and near[-1] + 1 < count:
            first = done.astype(BF16).astype(F32)
            second = (done - first).astype(BF16).astype(F32)
            third = done - first - second
            left = jnp.concatenate([first, first, second, first, third, second], axis=0).astype(BF16)
            right = jnp.concatenate([first, second, first, third, first, second], axis=0).astype(BF16)
            update = dot(left, right, ((0,), (0,)))
            for t in range(near[-1] + 1, count):
                tiles[t] = tiles[t] - update[SUBLANES * t : SUBLANES * (t + 1)]
        block = jnp.zeros_like(panel)
        for k in range(SUBLANES):
            block = jnp.where(lane == base + k, owned[k] * root, block)
        block = jnp.where(lane - base >= sub, block, 0.0)
        upper_ref[here, :] = jnp.where(lane >= base + SUBLANES, done, block)
        inverse_ref[here, :] = jnp.where(lane < base + SUBLANES, done, 0.0)
    first, second, third = thirds(inverse_ref[...])
    right = jnp.concatenate([jnp.concatenate([part] * 2, axis=1) for part in (first, second)], axis=0)
    both = dot(pieces_ref[:, : 2 * size], right, ((1,), (1,)))
    rest = dot(pieces_ref[:, size:], jnp.concatenate([third, first], axis=1), ((1,), (1,)))
    basis_ref[...] = both[:, :size] + (both[:, size:] + rest)
    projected_ref[0] = dot(mine_ref[...], inverse_ref[...], ((1,), (1,)), HIGHEST) * (1.0 / total**0.5)


def factor(packed, mine, sketch, total):
    rows, rank = sketch.shape
    return pl.pallas_call(
        functools.partial(factor_kernel, total),
        in_specs=[WHOLE] * 3,
        out_specs=(WHOLE,) * 3,
        out_shape=(
            jax.ShapeDtypeStruct(sketch.shape, F32),
            jax.ShapeDtypeStruct((rank, rank), F32),
            jax.ShapeDtypeStruct((1,) + mine.shape, F32),
        ),
        scratch_shapes=[pltpu.VMEM((rank, rank), F32), pltpu.VMEM((rows, 3 * rank), BF16)],
        compiler_params=pltpu.CompilerParams(vmem_limit_bytes=LIMIT),
        cost_estimate=cost(50 * 2 * rows * rank * rank, rows * rank, rows * rank),
        name="factor",
    )(packed, mine, sketch)


def exchange(parts, axis):
    return lax.all_to_all(parts, axis, 0, 0)


def body(samples, start_basis):
    rows, columns = samples.shape
    rank = start_basis.shape[1]
    y, x, cores, n_col = (lax.axis_size(name) for name in ("y", "x", "core", "col"))
    total = rows * y * x * cores
    share, gram = columns // (y * x * cores), gram_rows(rank)

    local, samples = sketch_product(samples, start_basis)
    chunks = sum_and_copy(exchange(local.reshape(n_col, rows // n_col, rank), "col"))
    sketch = exchange(chunks, "col").reshape(rows, rank)

    own, other = products(samples, sketch, share)
    others = lax.all_gather(other, "core", axis=0, tiled=True)
    trip = lambda parts, axis, n: exchange(parts.reshape(n, -1, 4, rank), axis).reshape(-1, rank)
    parts = trip(spread(own, others, share, x, gram), "x", x)
    parts = trip(respread(parts, share, x, y, gram), "y", y)
    mine, half = finish(parts, share, y, gram)
    packed = lax.all_gather(half, "core", axis=0, tiled=True)
    return factor(packed, mine, sketch, float(total))


def solution(mesh):
    split = jax.sharding.Mesh(mesh.devices.reshape(8, 4, 2, 8), ("y", "x", "core", "col"))
    row = ("y", "x", "core")
    in_specs = (P(row, "col"), P("col", None))
    out_specs = (P(row, None), P(), P("col", row, None))
    return jax.shard_map(body, mesh=split, in_specs=in_specs, out_specs=out_specs, check_vma=False)
```
